128 devices in a mesh: seq: 32 (over y, x, z_lo), tile: 4 (over z_hi, core).
Axes of the slice: x: 4, y: 4, z: 4 (z_hi: 2, z_lo: 2; z = z_hi * 2 + z_lo), core: 2. Of those that a mesh axis runs over, the one named last changes fastest.
Arguments:
- query_act: bfloat16 [2, 16, 64, 11520], P(None, None, 'seq', 'tile'), may hold values from -300 to 300
- key_act: bfloat16 [2, 16, 64, 11520], P(None, None, 'seq', 'tile'), may hold values from -10 to 10
- value_act: bfloat16 [2, 16, 64, 11520], P(None, None, 'seq', 'tile'), may hold values from -6 to 6
- residual: bfloat16 [2, 64, 160, 1152], P(None, 'seq', 'tile'), may hold values from -4 to 4
- gate_scale: float32 [1152], replicated, may hold values from 0.5 to 2
- w_out: bfloat16 [1152, 1152], replicated, may hold values from -0.1875 to 0.1875
- w_probe: float32 [1152, 256], replicated, may hold values from -0.1875 to 0.1875
- w_refine: float32 [3, 3, 256], replicated, may hold values from -0.125 to 0.125
- depth_bins: int32 [2, 256, 640], P(None, 'seq', 'tile'), may hold values from 0 to 255
- mom_probe: float32 [1152, 256], P(('seq', 'tile')), may hold values from -320 to 320
- var_probe: float32 [1152, 256], P(('seq', 'tile')), may hold values from 25 to 2500
- mom_refine: float32 [3, 3, 256], replicated, may hold values from -6144 to 6144
- var_refine: float32 [3, 3, 256], replicated, may hold values from 10000 to 1000000
Outputs:
- loss_map: float32 [2, 256, 640], P(None, 'seq', 'tile')
- map_grad: bfloat16 [2, 64, 160, 256], P(None, 'seq', 'tile')
- probe_step: float32 [1152, 256], P(('seq', 'tile'))
- refine_step: float32 [3, 3, 256], replicated
The draws below stay inside these ranges and needn't reach their ends.
All inputs are finite; a program needn't handle non-finite values.
Results may differ from the reference program's by a relative error of at most 0.019.
Values may be sent and summed in bfloat16 or wider, within the bound.
No kernel may reach another device: no remote copies, remote signals or barrier semaphores. Data moves between devices by JAX's collectives and lax.ppermute only.
A program may use at most 128 MiB of HBM per device.

```python
import math
import jax
import jax.numpy as jnp
from jax import lax

HEADS = 16
HD = 72
D = 1152
P_SIZE = 256
NBINS = 256
STEP = 10
FRAMES = 2
W = 160
H = 64


SCORE_LEVELS = (110.0, 170.0, 250.0, 330.0)


def attention_pair(key):
    spread = 1.6
    shape = (FRAMES, HEADS, H, W * HD)
    queries = spread * jax.random.truncated_normal(jax.random.fold_in(key, 101), -6.0, 6.0, shape, jnp.float32)
    key_field = spread * jax.random.truncated_normal(jax.random.fold_in(key, 102), -6.0, 6.0, shape, jnp.float32)
    aligned_q = queries
    aligned_k = key_field
    for frame_idx in range(FRAMES):
        row_picks = jax.random.randint(jax.random.fold_in(key, 200 + frame_idx), (12,), 0, H)
        col_picks = jax.random.randint(jax.random.fold_in(key, 300 + frame_idx), (12,), 0, W)
        for slot_idx in range(4):
            level = SCORE_LEVELS[slot_idx]
            chosen = lax.dynamic_slice(aligned_k, (frame_idx, 0, row_picks[3 * slot_idx + 1], col_picks[3 * slot_idx + 1] * HD), (1, HEADS, 1, HD))
            energy = jnp.maximum(jnp.sum(chosen * chosen, axis=3, keepdims=True), 0.5 * HD * spread * spread)
            factor = level * math.sqrt(HD) / energy
            aligned_q = lax.dynamic_update_slice(aligned_q, jnp.clip(factor * chosen, -300.0, 300.0), (frame_idx, 0, row_picks[3 * slot_idx], col_picks[3 * slot_idx] * HD))
            aligned_k = lax.dynamic_update_slice(aligned_k, chosen * (1.0 - 2.0 / level), (frame_idx, 0, row_picks[3 * slot_idx + 2], col_picks[3 * slot_idx + 2] * HD))
    return (queries, key_field)


def draw_query_act(key, part):
    shared = attention_pair(key)
    return shared[0].astype(jnp.bfloat16)


def draw_key_act(key, part):
    shared = attention_pair(key)
    return shared[1].astype(jnp.bfloat16)


def with_ends(drawn, stream_key, low, largest):
    longest = drawn.shape.index(max(drawn.shape))
    spots = []
    for shift in (0, 1):
        where = [jax.random.randint(jax.random.fold_in(stream_key, axis), (), 0, length) for axis, length in enumerate(drawn.shape)]
        where[longest] = (where[longest] + shift) % drawn.shape[longest]
        spots.append(tuple(where))
    return drawn.at[spots[0]].set(low).at[spots[1]].set(largest)


def levels(key, extent, pieces, low, top_value):
    def one(dim, blocks):
        steps = jax.random.uniform(jax.random.fold_in(jax.random.fold_in(key, 6), dim), (blocks,), jnp.float32, low / len(pieces), top_value / len(pieces))
        return jnp.repeat(jnp.exp(steps), extent[dim] // blocks).reshape((-1,) + (1,) * (len(extent) - dim - 1))

    level = one(*pieces[0])
    for cut in pieces[1:]:
        level = level * one(*cut)
    return level


def normal_values(stream_key, dims, deviation, bound, cuts=(), dtype=jnp.bfloat16):
    drawn = deviation * jax.random.normal(stream_key, dims, jnp.float32)
    if cuts:
        drawn = drawn * levels(stream_key, dims, cuts, -0.22, 0.18)
    return jnp.clip(drawn, -bound, bound).astype(dtype)


def setup_inputs(seed: int = 0) -> dict:
    key_list = jax.random.split(jax.random.key(seed), 14)
    return {
        "query_act": draw_query_act(jax.random.fold_in(key_list[13], 71), 0),
        "key_act": draw_key_act(jax.random.fold_in(key_list[13], 71), 0),
        "value_act": normal_values(key_list[2], (FRAMES, HEADS, H, W * HD), 1.0, 6.0, ((2, 32), (3, 4))),
        "residual": normal_values(key_list[3], (FRAMES, H, W, D), 0.3, 4.0, ((1, 32), (2, 4))),
        "gate_scale": jnp.clip(jax.random.uniform(key_list[4], (D,), jnp.float32, 0.5, 2.0), 0.5, 2.0),
        "w_out": normal_values(key_list[5], (D, D), D ** -0.5, 0.1875),
        "w_probe": normal_values(key_list[6], (D, P_SIZE), D ** -0.5, 0.1875, (), jnp.float32),
        "w_refine": normal_values(key_list[7], (3, 3, P_SIZE), (9 * P_SIZE) ** -0.5, 0.125, (), jnp.float32),
        "depth_bins": with_ends(jax.random.randint(key_list[8], (FRAMES, 4 * H, 4 * W), 0, NBINS), jax.random.fold_in(key_list[8], 1), 0, NBINS - 1).astype(jnp.int32),
        "mom_probe": normal_values(key_list[9], (D, P_SIZE), 50.0, 320.0, ((0, 128),), jnp.float32),
        "var_probe": jnp.clip(jnp.exp(math.log(2500.0) - 4.6051702 * jax.random.uniform(key_list[10], (D, P_SIZE), jnp.float32) ** levels(key_list[10], (D, P_SIZE), ((0, 128),), -0.2, 0.2)), 25.0, 2500.0),
        "mom_refine": normal_values(key_list[11], (3, 3, P_SIZE), 1000.0, 6144.0, (), jnp.float32),
        "var_refine": jnp.clip(jnp.exp(jax.random.uniform(key_list[12], (3, 3, P_SIZE), jnp.float32, math.log(10000.0), math.log(1000000))), 10000.0, 1000000),
    }


BETA_ONE = 0.9
BETA_TWO = 0.999
ADAM_EPS = 1e-08
NORM_EPS = 1e-06
PRECISE = lax.Precision.HIGHEST

def interp_weights(pixel, latent, count_in):
    source = (pixel + 0.5) * 0.25 - 0.5
    offset = source[:, None] - latent[None, :]
    weight = jnp.maximum(0.0, 1.0 - jnp.abs(offset))
    weight = weight + jnp.where(latent[None, :] == 0.0, jnp.maximum(0.0, 1.0 - jnp.abs(offset + 1.0)), 0.0)
    weight = weight + jnp.where(latent[None, :] == count_in - 1.0, jnp.maximum(0.0, 1.0 - jnp.abs(offset - 1.0)), 0.0)
    inside = (pixel[:, None] >= 0.0) & (pixel[:, None] < 4.0 * count_in) & (latent[None, :] >= 0.0) & (latent[None, :] < count_in)
    return jnp.where(inside, weight, 0.0)

def refine_taps(upsampled, w_refine, out_rows, out_cols):
    tap_maps = jnp.einsum('fqwp,abp->fabqw', upsampled, w_refine, precision=PRECISE)
    depth = tap_maps[:, 0, 0, :out_rows, :out_cols]
    for tap_row in range(3):
        for tap_col in range(3):
            if tap_row + tap_col > 0:
                depth = depth + tap_maps[:, tap_row, tap_col, tap_row:tap_row + out_rows, tap_col:tap_col + out_cols]
    return depth

def adam_step(grad, moment, second):
    new_moment = BETA_ONE * moment + (1.0 - BETA_ONE) * grad
    new_second = BETA_TWO * second + (1.0 - BETA_TWO) * grad * grad
    return new_moment / (1.0 - BETA_ONE ** STEP) / (jnp.sqrt(new_second / (1.0 - BETA_TWO ** STEP)) + ADAM_EPS)

def attend_item(item):
    query_rows, key_rows, value_rows = item
    block_rows = W * math.gcd(H, 16)

    def one_block(query_block):
        scores = jnp.dot(query_block, key_rows.T, preferred_element_type=jnp.float32) * HD ** (-0.5)
        row_top = lax.optimization_barrier(jnp.max(scores, axis=1, keepdims=True))
        shifted = jnp.exp(scores - row_top)
        row_total = lax.optimization_barrier(jnp.sum(shifted, axis=1, keepdims=True))
        weights = shifted.astype(jnp.bfloat16)
        summed = jnp.dot(weights, value_rows, preferred_element_type=jnp.float32)
        return (summed / row_total).astype(jnp.bfloat16)
    blocks = query_rows.reshape(-1, block_rows, HD)
    return lax.map(one_block, blocks).reshape(-1, HD)

def reference(query_act, key_act, value_act, residual, gate_scale, w_out, w_probe, w_refine, depth_bins, mom_probe, var_probe, mom_refine, var_refine):
    items = FRAMES * HEADS
    query_items = query_act.reshape(items, H * W, HD)
    key_items = key_act.reshape(items, H * W, HD)
    value_items = value_act.reshape(items, H * W, HD)
    attended = lax.map(attend_item, (query_items, key_items, value_items))
    attended = attended.reshape(FRAMES, HEADS, H, W, HD)
    mixed = jnp.einsum('fhrcd,hde->frce', attended.astype(jnp.float32), w_out.reshape(HEADS, HD, D).astype(jnp.float32), precision=PRECISE)
    stream = residual.astype(jnp.float32) + gate_scale * mixed
    row_mean = lax.optimization_barrier(jnp.mean(stream, axis=3, keepdims=True))
    centered = stream - row_mean
    row_var = lax.optimization_barrier(jnp.mean(centered * centered, axis=3, keepdims=True))
    features = (centered * lax.rsqrt(row_var + NORM_EPS)).astype(jnp.bfloat16)
    probe_bf = w_probe.astype(jnp.bfloat16)
    probe_map = jnp.dot(features.reshape(-1, D), probe_bf, preferred_element_type=jnp.float32).astype(jnp.bfloat16)
    probe_map = probe_map.reshape(FRAMES, H, W, P_SIZE)
    row_weights = interp_weights(jnp.arange(4 * H).astype(jnp.float32), jnp.arange(H).astype(jnp.float32), float(H))
    col_weights = interp_weights(jnp.arange(4 * W).astype(jnp.float32), jnp.arange(W).astype(jnp.float32), float(W))
    up_rows = jnp.einsum('qr,frcp->fqcp', row_weights, probe_map.astype(jnp.float32), precision=PRECISE)
    upsampled = jnp.einsum('wc,fqcp->fqwp', col_weights, up_rows, precision=PRECISE)
    padded_up = jnp.pad(upsampled, ((0, 0), (1, 1), (1, 1), (0, 0)))
    depth = refine_taps(padded_up, w_refine, 4 * H, 4 * W)
    target = (depth_bins.astype(jnp.float32) + 0.5) * (4.0 / NBINS) - 2.0
    depth_error = depth - target
    loss_map = depth_error * depth_error
    depth_grad = 2.0 * depth_error
    refine_grad = jnp.stack([jnp.stack([jnp.einsum('fyx,fyxp->p', depth_grad, padded_up[:, tap_row:tap_row + 4 * H, tap_col:tap_col + 4 * W], precision=PRECISE) for tap_col in range(3)]) for tap_row in range(3)])
    grad_pad = jnp.pad(depth_grad, ((0, 0), (1, 1), (1, 1)))
    shifted_grad = jnp.stack([jnp.stack([grad_pad[:, 2 - tap_row:2 - tap_row + 4 * H, 2 - tap_col:2 - tap_col + 4 * W] for tap_col in range(3)], axis=1) for tap_row in range(3)], axis=1)
    up_grad = jnp.einsum('fabqw,abp->fqwp', shifted_grad, w_refine, precision=PRECISE)
    grad_rows = jnp.einsum('qr,fqwp->frwp', row_weights, up_grad, precision=PRECISE)
    map_grad = jnp.einsum('wc,frwp->frcp', col_weights, grad_rows, precision=PRECISE).astype(jnp.bfloat16)
    probe_grad = jnp.dot(features.reshape(-1, D).T, map_grad.reshape(-1, P_SIZE), preferred_element_type=jnp.float32)
    probe_step = adam_step(probe_grad, mom_probe, var_probe)
    refine_step = adam_step(refine_grad, mom_refine, var_refine)
    return (loss_map, map_grad, probe_step, refine_step)
```

```python
import functools
import math

import jax
import jax.numpy as jnp
from jax import lax
from jax.experimental import pallas as pl
from jax.experimental.pallas import tpu as pltpu
from jax.sharding import Mesh, PartitionSpec as P

HD = 72
HEADS = 16
D = 1152
P_SIZE = 256
NBINS = 256
STEP = 10
ROWS = 64
COLS = 40
TOKENS = ROWS * COLS
BLOCK = 256
SEQ_COUNT = 32
TILE_COUNT = 4
FULL_ROWS = 256
FULL_COLS = 640

BETA_ONE = 0.9
BETA_TWO = 0.999
ADAM_EPS = 1e-08
NORM_EPS = 1e-06
PRECISE = lax.Precision.HIGHEST
EXP_SCALE = HD ** (-0.5) * math.log2(math.e)

SEQ = ("y", "x", "z_lo")
TILE = ("z_hi", "core")
PLANE = ("y", "x")
COLUMN = ("z_lo", "z_hi", "core")

NT = (((1,), (1,)), ((), ()))
TN = (((0,), (0,)), ((), ()))
F32 = jnp.float32
BF16 = jnp.bfloat16
VMEM = pl.BlockSpec(memory_space=pltpu.VMEM)
SMEM = pl.BlockSpec(memory_space=pltpu.SMEM)


def call(kernel, out_shape, operands, scratch=(), flops=0, bytes_accessed=0, transcendentals=0, limit=56):
    in_specs = [SMEM if x.dtype == jnp.int32 and x.ndim == 1 else VMEM for x in operands]
    many = isinstance(out_shape, (list, tuple))
    return pl.pallas_call(
        kernel,
        out_shape=out_shape,
        in_specs=in_specs,
        out_specs=[VMEM] * len(out_shape) if many else VMEM,
        scratch_shapes=list(scratch),
        compiler_params=pltpu.CompilerParams(vmem_limit_bytes=limit * 2**20),
        cost_estimate=pl.CostEstimate(
            flops=flops, bytes_accessed=bytes_accessed, transcendentals=transcendentals
        ),
    )(*operands)


def halves(value):
    high = value.astype(BF16)
    low = (value - high.astype(F32)).astype(BF16)
    return high, low


def unpack(packed, rows):
    for c in range(COLS):
        rows[c * ROWS : (c + 1) * ROWS, :HD] = packed[:, c * HD : (c + 1) * HD]


def attend_kernel(first, last, *refs):
    if first:
        q_ref, kv_ref, query_rows, acc_out, key_rows, value_rows, scores_ref = refs
        query_rows[...] = jnp.zeros_like(query_rows)
        unpack(q_ref, query_rows)
    elif last:
        query_rows, kv_ref, acc_ref, out_ref, key_rows, value_rows, scores_ref, acc_out = refs
    else:
        query_rows, kv_ref, acc_ref, acc_out, key_rows, value_rows, scores_ref = refs
    key_rows[...] = jnp.zeros_like(key_rows)
    lane = lax.broadcasted_iota(jnp.int32, (TOKENS, 128), 1)
    value_rows[...] = jnp.where(lane == HD, 1.0, 0.0).astype(BF16)
    unpack(kv_ref.at[0], key_rows)
    unpack(kv_ref.at[1], value_rows)
    blocks = TOKENS // BLOCK
    block_lane = lax.broadcasted_iota(jnp.int32, (BLOCK, 128), 1)

    def scores(i):
        rows = pl.ds(pl.multiple_of(i * BLOCK, BLOCK), BLOCK)
        return lax.dot_general(query_rows[rows, :], key_rows[...], NT, preferred_element_type=F32)

    def step(i, now, later):
        scores_ref[later] = scores(jnp.minimum(i + 1, blocks - 1))
        rows = pl.ds(pl.multiple_of(i * BLOCK, BLOCK), BLOCK)
        block = scores_ref[now]
        top = jnp.max(block, axis=1, keepdims=True)
        if not first:
            old = acc_ref[rows, :]
            old_top = old[:, HD + 1 : HD + 2]
            top = jnp.maximum(top, old_top)
        weights = jnp.exp2((block - top) * EXP_SCALE).astype(BF16)
        total = jnp.dot(weights, value_rows[...], preferred_element_type=F32)
        if not first:
            total = total + old * jnp.exp2((old_top - top) * EXP_SCALE)
        if last:
            acc_out[rows, :] = total / total[:, HD : HD + 1]
        else:
            acc_out[rows, :] = jnp.where(block_lane == HD + 1, top, total)

    scores_ref[0] = scores(0)

    def pair(j, carry):
        step(2 * j, 0, 1)
        step(2 * j + 1, 1, 0)
        return carry

    lax.fori_loop(0, blocks // 2, pair, 0)
    if last:
        for c in range(COLS):
            out_ref[:, c * HD : (c + 1) * HD] = acc_out[c * ROWS : (c + 1) * ROWS, :HD].astype(BF16)


def attend(first, last, *operands):
    rows = jax.ShapeDtypeStruct((TOKENS, 128), BF16)
    acc = jax.ShapeDtypeStruct((TOKENS, 128), F32)
    if first:
        out = [rows, acc]
    elif last:
        out = jax.ShapeDtypeStruct((ROWS, COLS * HD), BF16)
    else:
        out = acc
    scratch = [
        pltpu.VMEM((TOKENS, 128), BF16),
        pltpu.VMEM((TOKENS, 128), BF16),
        pltpu.VMEM((2, BLOCK, TOKENS), F32),
    ]
    if last:
        scratch.append(pltpu.VMEM((TOKENS, 128), F32))
    return call(
        functools.partial(attend_kernel, first, last),
        out,
        operands,
        scratch,
        flops=4 * TOKENS * TOKENS * 256,
        bytes_accessed=4 * 2**20,
        transcendentals=TOKENS * TOKENS,
    )


def weights_kernel(w_probe, taps, probe_out, tap_weights):
    probe = w_probe[...].astype(BF16)
    probe_out[...] = probe
    high, low = halves(taps[...])
    rest = (taps[...] - high.astype(F32) - low.astype(F32)).astype(BF16)
    folded = lax.dot_general(
        jnp.concatenate([high, low, rest], 0).astype(BF16), probe, NT, preferred_element_type=F32
    )
    folded = folded[:24] + folded[24:48] + folded[48:72]
    tap_high, tap_low = halves(folded)
    tap_weights[...] = jnp.concatenate([tap_high.astype(F32), tap_low.astype(F32)], 0).astype(BF16)


def features_kernel(
    merged, residual, gate, w_out, tap_weights, bins, features_out, tap_maps, spread, joined
):
    for c in range(COLS):
        spread[c * ROWS : (c + 1) * ROWS, :HD] = merged[:, c * HD : (c + 1) * HD].astype(F32)
    for h in range(HEADS):
        for g in range(4):
            f, r = divmod(g, 2)
            piece = spread[pl.ds(f * 2 * HEADS + h * 2 + r, COLS, stride=ROWS), :]
            joined[g * COLS : (g + 1) * COLS, h * HD : (h + 1) * HD] = piece[:, :HD]
    mixed = jnp.dot(joined[...].astype(BF16), w_out[...], preferred_element_type=F32)
    stream = residual[...].astype(F32) + gate[...] * mixed
    centered = stream - jnp.mean(stream, axis=1, keepdims=True)
    var = jnp.mean(centered * centered, axis=1, keepdims=True)
    features = (centered * lax.rsqrt(var + NORM_EPS)).astype(BF16)
    features_out[...] = features
    maps = lax.dot_general(tap_weights[...], features, NT, preferred_element_type=F32)
    maps = maps[:24] + maps[24:48]
    tap_maps[...] = jnp.zeros_like(tap_maps)
    for g in range(4):
        for b in range(3):
            tap_maps[g * 8 : (g + 1) * 8, b * 128 : b * 128 + COLS] = maps[
                b * 8 : (b + 1) * 8, g * COLS : (g + 1) * COLS
            ]
    tap_maps[32:48, :160] = bins[...].astype(F32)


def hat(offset):
    return jnp.maximum(0.0, 1.0 - jnp.abs(offset))


def interp(pixel, latent, count_in):
    source = (pixel.astype(F32) + 0.5) * 0.25 - 0.5
    offset = source - latent.astype(F32)
    weight = hat(offset)
    weight = weight + jnp.where(latent == 0, hat(offset + 1.0), 0.0)
    weight = weight + jnp.where(latent == count_in - 1, hat(offset - 1.0), 0.0)
    inside = (pixel >= 0) & (pixel < 4 * count_in) & (latent >= 0) & (latent < count_in)
    return jnp.where(inside, weight, 0.0)


def col_weights(tile, source):
    shape = (384, 256)
    i = lax.broadcasted_iota(jnp.int32, shape, 0)
    x = lax.broadcasted_iota(jnp.int32, shape, 1)
    tap = i >> 7
    c = i & 127
    weight = interp(tile * 160 - 4 + x + tap, source * COLS + c, TILE_COUNT * COLS)
    return jnp.where(c < COLS, weight, 0.0)


def row_weights(seq, source):
    shape = (32, 32)
    i = lax.broadcasted_iota(jnp.int32, shape, 0)
    j = lax.broadcasted_iota(jnp.int32, shape, 1)
    y = i & 15
    tap = j & 7
    weight = interp(seq * 8 - 4 + y + tap, source * 2 + ((j >> 3) & 1), ROWS)
    return jnp.where(((i >> 4) == (j >> 4)) & (tap < 3), weight, 0.0)


def dot(left, right, dims=None):
    if dims is None:
        dims = (((1,), (0,)), ((), ()))
    return lax.dot_general(left, right, dims, precision=PRECISE, preferred_element_type=F32)


def pick(shape, wanted, there):
    i = lax.broadcasted_iota(jnp.int32, shape, 0)
    j = lax.broadcasted_iota(jnp.int32, shape, 1)
    return jnp.where(wanted(i) == there(j), 1.0, 0.0).astype(BF16)


def widen_kernel(place, own, near, far, out):
    tile = place[1]
    maps = jnp.zeros((32, 256), F32)
    bins = jnp.zeros((16, 256), F32)
    for block, source in ((own, tile), (near, place[3]), (far, place[5])):
        maps = maps + dot(block[:32, :], col_weights(tile, source))
        move = pick((160, 256), lambda i: source * 160 + i, lambda j: tile * 160 - 3 + j)
        bins = bins + jnp.dot(
            block[32:48, :160].astype(BF16), move, preferred_element_type=F32
        )
    out[:32, :] = maps
    out[32:48, :] = bins


def loss_kernel(
    place, own, near, far, features, taps, probe, loss_out, map_grad, parts, token_grad
):
    seq, tile = place[0], place[1]
    own_rows = row_weights(seq, seq)
    depth = jnp.zeros((32, 256), F32)
    bins = jnp.zeros((32, 256), F32)
    for block, source in ((own, seq), (near, place[2]), (far, place[4])):
        depth = depth + dot(row_weights(seq, source), block[:32, :])
        move = pick(
            (32, 16),
            lambda i: (i >> 4) * 1024 + seq * 8 - 3 + (i & 15),
            lambda j: (j >> 3) * 1024 + source * 8 + (j & 7),
        )
        bins = bins + jnp.dot(move, block[32:48, :].astype(BF16), preferred_element_type=F32)
    target = (bins + 0.5) * (4.0 / NBINS) - 2.0
    error = depth - target
    loss = error * error
    for f in range(2):
        loss_out[f] = loss[f * 16 + 3 : f * 16 + 11, 3:163]
    y = lax.broadcasted_iota(jnp.int32, (32, 256), 0) & 15
    x = lax.broadcasted_iota(jnp.int32, (32, 256), 1)
    row = seq * 8 - 3 + y
    col = tile * 160 - 3 + x
    valid = (y < 14) & (x < 166) & (row >= 0) & (row < FULL_ROWS) & (col >= 0) & (col < FULL_COLS)
    grad = jnp.where(valid, 2.0 * error, 0.0)
    narrow = dot(own_rows, grad, TN)
    narrow = dot(narrow, col_weights(tile, tile), NT)
    for g in range(4):
        for b in range(3):
            token_grad[b * 8 : (b + 1) * 8, g * COLS : (g + 1) * COLS] = narrow[
                g * 8 : (g + 1) * 8, b * 128 : b * 128 + COLS
            ]
    grads = token_grad[...]
    map_grad[...] = dot(grads, taps[...], TN).astype(BF16)
    high, low = halves(grads)
    feature_grad = jnp.dot(high, features[...], preferred_element_type=F32) + jnp.dot(
        low, features[...], preferred_element_type=F32
    )
    high, low = halves(feature_grad)
    refine = jnp.dot(high, probe[...], preferred_element_type=F32) + jnp.dot(
        low, probe[...], preferred_element_type=F32
    )
    parts[...] = jnp.zeros_like(parts)
    for j in range(16):
        parts[j, :, :P_SIZE] = refine
        parts[j, :, P_SIZE : P_SIZE + 72] = feature_grad[:, j * 72 : (j + 1) * 72]


def plane_sum_kernel(parts, out):
    total = jnp.sum(parts[...], axis=0)
    out[...] = jnp.zeros_like(out)
    for z in range(8):
        out[z, :, :P_SIZE] = total[:, :P_SIZE]
        out[z, :, P_SIZE : P_SIZE + 9] = total[:, P_SIZE + z * 9 : P_SIZE + (z + 1) * 9]


def adam_step(grad, moment, second):
    new_moment = BETA_ONE * moment + (1.0 - BETA_ONE) * grad
    new_second = BETA_TWO * second + (1.0 - BETA_TWO) * grad * grad
    return (
        new_moment
        / (1.0 - BETA_ONE**STEP)
        / (jnp.sqrt(new_second / (1.0 - BETA_TWO**STEP)) + ADAM_EPS)
    )


def step_kernel(parts, taps, mom_probe, var_probe, mom_refine, var_refine, probe_out, refine_out):
    total = jnp.sum(parts[...], axis=0)
    probe_grad = dot(total[:, P_SIZE:], taps[...], TN)
    probe_out[...] = adam_step(probe_grad[:9], mom_probe[...], var_probe[...])
    for a in range(3):
        for b in range(3):
            refine_out[a, b : b + 1] = adam_step(
                total[b * 8 + a : b * 8 + a + 1, :P_SIZE],
                mom_refine[a, b : b + 1],
                var_refine[a, b : b + 1],
            )


def body(
    query_act,
    key_act,
    value_act,
    residual,
    gate_scale,
    w_out,
    w_probe,
    w_refine,
    depth_bins,
    mom_probe,
    var_probe,
    mom_refine,
    var_refine,
):
    seq = lax.axis_index(SEQ)
    tile = lax.axis_index(TILE)
    odd_seq = seq & 1
    odd_tile = tile & 1
    far_seq = seq + 2 * odd_seq - 1
    far_tile = tile + 2 * odd_tile - 1
    place = jnp.stack([seq, tile, seq ^ 1, tile ^ 1, far_seq, far_tile]).astype(jnp.int32)

    taps = jnp.pad(w_refine.transpose(1, 0, 2), ((0, 0), (0, 5), (0, 0))).reshape(24, P_SIZE)
    probe, tap_weights = call(
        weights_kernel,
        [jax.ShapeDtypeStruct((D, P_SIZE), BF16), jax.ShapeDtypeStruct((48, D), BF16)],
        (w_probe, taps),
        limit=16,
    )

    def split(act):
        return act.reshape(SEQ_COUNT, 1, 2, COLS * HD)

    sent = jnp.concatenate([split(query_act), split(key_act), split(value_act)], axis=1)
    here = lax.all_to_all(sent, SEQ, split_axis=0, concat_axis=0, tiled=True)
    queries = here[:, 0].reshape(ROWS, COLS * HD)
    own_kv = jnp.stack([here[:, i].reshape(ROWS, COLS * HD) for i in (1, 2)])
    swap_core = [(0, 1), (1, 0)]
    z_kv = lax.ppermute(own_kv, "z_hi", swap_core)
    core_kv = lax.ppermute(own_kv, "core", swap_core)
    query_rows, acc = attend(True, False, queries, own_kv)
    acc = attend(False, False, query_rows, core_kv, acc)
    z_core_kv = lax.ppermute(z_kv, "core", swap_core)
    acc = attend(False, False, query_rows, z_kv, acc)
    attended = attend(False, True, query_rows, z_core_kv, acc)
    merged = lax.all_to_all(
        attended.reshape(SEQ_COUNT, 2, COLS * HD), SEQ, split_axis=0, concat_axis=0, tiled=True
    ).reshape(ROWS, COLS * HD)

    features, tap_maps = call(
        features_kernel,
        [jax.ShapeDtypeStruct((160, D), BF16), jax.ShapeDtypeStruct((48, 384), F32)],
        (merged, residual.reshape(160, D), gate_scale.reshape(1, D), w_out, tap_weights, depth_bins.reshape(16, 160)),
        [pltpu.VMEM((TOKENS, 128), F32), pltpu.VMEM((160, D), F32)],
        limit=32,
    )
    tile_far = [(1, 2), (2, 1)]
    seq_near = [(i, i ^ 1) for i in range(SEQ_COUNT)]
    seq_far = [(i, i + 2 * (i & 1) - 1) for i in range(1, SEQ_COUNT - 1)]
    wide = call(
        widen_kernel,
        jax.ShapeDtypeStruct((48, 256), F32),
        (
            place,
            tap_maps,
            lax.ppermute(tap_maps, "core", swap_core),
            lax.ppermute(tap_maps, TILE, tile_far),
        ),
        limit=16,
    )
    loss_map, map_grad, parts = call(
        loss_kernel,
        [
            jax.ShapeDtypeStruct((2, 8, 160), F32),
            jax.ShapeDtypeStruct((160, P_SIZE), BF16),
            jax.ShapeDtypeStruct((16, 24, 384), F32),
        ],
        (
            place,
            wide,
            lax.ppermute(wide, SEQ, seq_near),
            lax.ppermute(wide, SEQ, seq_far),
            features,
            taps,
            probe,
        ),
        [pltpu.VMEM((24, 160), F32)],
        limit=16,
    )
    parts = lax.all_to_all(parts, PLANE, split_axis=0, concat_axis=0, tiled=True)
    parts = call(plane_sum_kernel, jax.ShapeDtypeStruct((8, 24, 384), F32), (parts,), limit=16)
    parts = lax.all_to_all(parts, COLUMN, split_axis=0, concat_axis=0, tiled=True)
    probe_step, refine_step = call(
        step_kernel,
        [
            jax.ShapeDtypeStruct((9, P_SIZE), F32),
            jax.ShapeDtypeStruct((3, 3, P_SIZE), F32),
        ],
        (parts, taps, mom_probe, var_probe, mom_refine, var_refine),
        limit=16,
    )
    return (loss_map, map_grad.reshape(2, 2, COLS, P_SIZE), probe_step, refine_step)


def solution(mesh):
    fine = Mesh(mesh.devices.reshape(4, 4, 2, 2, 2), ("y", "x", "z_lo", "z_hi", "core"))
    slab = (*SEQ, *TILE)
    in_specs = (
        P(None, None, SEQ, TILE),
        P(None, None, SEQ, TILE),
        P(None, None, SEQ, TILE),
        P(None, SEQ, TILE, None),
        P(),
        P(),
        P(),
        P(),
        P(None, SEQ, TILE),
        P(slab, None),
        P(slab, None),
        P(),
        P(),
    )
    out_specs = (
        P(None, SEQ, TILE),
        P(None, SEQ, TILE, None),
        P(slab, None),
        P(),
    )
    return jax.shard_map(body, mesh=fine, in_specs=in_specs, out_specs=out_specs, check_vma=False)
```

```python
import functools
import math

import jax
import jax.numpy as jnp
from jax import lax
from jax.experimental import pallas as pl
from jax.experimental.pallas import tpu as pltpu
from jax.sharding import Mesh, PartitionSpec as P

HD = 72
HEADS = 16
D = 1152
P_SIZE = 256
NBINS = 256
STEP = 10
ROWS = 64
COLS = 40
TOKENS = ROWS * COLS
BLOCK = 512
SEQ_COUNT = 32
TILE_COUNT = 4
FULL_ROWS = 256
FULL_COLS = 640

BETA_ONE = 0.9
BETA_TWO = 0.999
ADAM_EPS = 1e-08
NORM_EPS = 1e-06
PRECISE = lax.Precision.HIGHEST
EXP_SCALE = HD ** (-0.5) * math.log2(math.e)

SEQ = ("y", "x", "z_lo")
TILE = ("z_hi", "core")
PLANE = ("y", "x")
COLUMN = ("z_lo", "z_hi", "core")

NT = (((1,), (1,)), ((), ()))
TN = (((0,), (0,)), ((), ()))
F32 = jnp.float32
BF16 = jnp.bfloat16
VMEM = pl.BlockSpec(memory_space=pltpu.VMEM)
SMEM = pl.BlockSpec(memory_space=pltpu.SMEM)


def call(
    kernel,
    out_shape,
    operands,
    scratch=(),
    flops=0,
    bytes_accessed=0,
    transcendentals=0,
    limit=56,
    left=0,
):
    in_specs = [SMEM if x.dtype == jnp.int32 and x.ndim == 1 else VMEM for x in operands]
    for i in range(len(operands) - left, len(operands)):
        in_specs[i] = pl.BlockSpec(memory_space=pl.ANY)
    many = isinstance(out_shape, (list, tuple))
    return pl.pallas_call(
        kernel,
        out_shape=out_shape,
        in_specs=in_specs,
        out_specs=[VMEM] * len(out_shape) if many else VMEM,
        scratch_shapes=list(scratch),
        compiler_params=pltpu.CompilerParams(vmem_limit_bytes=limit * 2**20),
        cost_estimate=pl.CostEstimate(
            flops=flops, bytes_accessed=bytes_accessed, transcendentals=transcendentals
        ),
    )(*operands)


def halves(value):
    high = value.astype(BF16)
    low = (value - high.astype(F32)).astype(BF16)
    return high, low


def unpack(packed, rows):
    for c in range(COLS):
        rows[c * ROWS : (c + 1) * ROWS, :HD] = packed[:, c * HD : (c + 1) * HD]


def attend_kernel(first, last, *refs):
    if first:
        q_ref, kv_ref, query_rows, acc_out, key_rows, value_rows, scores_ref = refs
        query_rows[...] = jnp.zeros_like(query_rows)
        unpack(q_ref, query_rows)
    elif last:
        query_rows, kv_ref, acc_ref, out_ref, key_rows, value_rows, scores_ref, acc_out = refs
    else:
        query_rows, kv_ref, acc_ref, acc_out, key_rows, value_rows, scores_ref = refs
    key_rows[...] = jnp.zeros_like(key_rows)
    lane = lax.broadcasted_iota(jnp.int32, (TOKENS, 128), 1)
    value_rows[...] = jnp.where(lane == HD, 1.0, 0.0).astype(BF16)
    unpack(kv_ref.at[0], key_rows)
    unpack(kv_ref.at[1], value_rows)

    def block_rows(i):
        return pl.ds(pl.multiple_of(i * BLOCK, BLOCK), BLOCK)

    def scores(i, slot):
        scores_ref[slot] = lax.dot_general(
            query_rows[block_rows(i), :], key_rows[...], NT, preferred_element_type=F32
        )

    def finish(i, slot):
        rows = block_rows(i)
        block = scores_ref[slot]
        top = jnp.max(block, axis=1, keepdims=True)
        if not first:
            old = acc_ref[rows, :]
            old_top = old[:, HD + 1 : HD + 2]
            top = jnp.maximum(top, old_top)
        weights = jnp.exp2((block - top) * EXP_SCALE).astype(BF16)
        total = jnp.dot(weights, value_rows[...], preferred_element_type=F32)
        if not first:
            total = total + old * jnp.exp2((old_top - top) * EXP_SCALE)
        if last:
            acc_out[rows, :] = total / total[:, HD : HD + 1]
        else:
            block_lane = lax.broadcasted_iota(jnp.int32, (BLOCK, 128), 1)
            acc_out[rows, :] = jnp.where(block_lane == HD + 1, top, total)

    def pair(j, carry):
        scores(2 * j + 1, 1)
        finish(2 * j, 0)
        scores(2 * j + 2, 0)
        finish(2 * j + 1, 1)
        return carry

    scores(0, 0)
    lax.fori_loop(0, TOKENS // BLOCK // 2, pair, 0)
    finish(TOKENS // BLOCK - 1, 0)
    if last:
        for c in range(COLS):
            out_ref[:, c * HD : (c + 1) * HD] = acc_out[c * ROWS : (c + 1) * ROWS, :HD].astype(BF16)


def attend(first, last, *operands):
    rows = jax.ShapeDtypeStruct((TOKENS, 128), BF16)
    acc = jax.ShapeDtypeStruct((TOKENS, 128), F32)
    if first:
        out = [rows, acc]
    elif last:
        out = jax.ShapeDtypeStruct((ROWS, COLS * HD), BF16)
    else:
        out = acc
    scratch = [
        pltpu.VMEM((TOKENS, 128), BF16),
        pltpu.VMEM((TOKENS, 128), BF16),
        pltpu.VMEM((2, BLOCK, TOKENS), F32),
    ]
    if last:
        scratch.append(pltpu.VMEM((TOKENS, 128), F32))
    return call(
        functools.partial(attend_kernel, first, last),
        out,
        operands,
        scratch,
        flops=4 * TOKENS * TOKENS * 256,
        bytes_accessed=4 * 2**20,
        transcendentals=TOKENS * TOKENS,
        limit=24,
    )


def weights_kernel(w_probe, taps, bins, probe_out, tap_weights, bins_out):
    bins_out[...] = bins[...].astype(F32)
    probe = w_probe[...].astype(BF16)
    probe_out[...] = probe
    high, low = halves(taps[...])
    rest = (taps[...] - high.astype(F32) - low.astype(F32)).astype(BF16)
    folded = lax.dot_general(
        jnp.concatenate([high, low, rest], 0).astype(BF16), probe, NT, preferred_element_type=F32
    )
    folded = folded[:24] + folded[24:48] + folded[48:72]
    tap_high, tap_low = halves(folded)
    tap_weights[...] = jnp.concatenate([tap_high.astype(F32), tap_low.astype(F32)], 0).astype(BF16)


def features_kernel(
    merged, residual, gate, w_out, tap_weights, bins, features_out, tap_maps, spread, joined
):
    for c in range(COLS):
        spread[c * ROWS : (c + 1) * ROWS, :HD] = merged[:, c * HD : (c + 1) * HD].astype(F32)
    for h in range(HEADS):
        for g in range(4):
            f, r = divmod(g, 2)
            piece = spread[pl.ds(f * 2 * HEADS + h * 2 + r, COLS, stride=ROWS), :]
            joined[g * COLS : (g + 1) * COLS, h * HD : (h + 1) * HD] = piece[:, :HD]
    mixed = jnp.dot(joined[...].astype(BF16), w_out[...], preferred_element_type=F32)
    stream = residual[...].astype(F32) + gate[...] * mixed
    centered = stream - jnp.mean(stream, axis=1, keepdims=True)
    var = jnp.mean(centered * centered, axis=1, keepdims=True)
    features = (centered * lax.rsqrt(var + NORM_EPS)).astype(BF16)
    features_out[...] = features
    maps = lax.dot_general(tap_weights[...], features, NT, preferred_element_type=F32)
    maps = maps[:24] + maps[24:48]
    tap_maps[...] = jnp.zeros_like(tap_maps)
    for g in range(4):
        for b in range(3):
            tap_maps[g * 8 : (g + 1) * 8, b * 128 : b * 128 + COLS] = maps[
                b * 8 : (b + 1) * 8, g * COLS : (g + 1) * COLS
            ]
    tap_maps[32:48, :160] = bins[...]


def hat(offset):
    return jnp.maximum(0.0, 1.0 - jnp.abs(offset))


def interp(pixel, latent, count_in):
    source = (pixel.astype(F32) + 0.5) * 0.25 - 0.5
    offset = source - latent.astype(F32)
    weight = hat(offset)
    weight = weight + jnp.where(latent == 0, hat(offset + 1.0), 0.0)
    weight = weight + jnp.where(latent == count_in - 1, hat(offset - 1.0), 0.0)
    inside = (pixel >= 0) & (pixel < 4 * count_in) & (latent >= 0) & (latent < count_in)
    return jnp.where(inside, weight, 0.0)


def col_weights(tile, source):
    shape = (384, 256)
    i = lax.broadcasted_iota(jnp.int32, shape, 0)
    x = lax.broadcasted_iota(jnp.int32, shape, 1)
    tap = i >> 7
    c = i & 127
    weight = interp(tile * 160 - 4 + x + tap, source * COLS + c, TILE_COUNT * COLS)
    return jnp.where(c < COLS, weight, 0.0).astype(BF16)


def row_weights(seq, source):
    shape = (32, 32)
    i = lax.broadcasted_iota(jnp.int32, shape, 0)
    j = lax.broadcasted_iota(jnp.int32, shape, 1)
    y = i & 15
    tap = j & 7
    weight = interp(seq * 8 - 4 + y + tap, source * 2 + ((j >> 3) & 1), ROWS)
    return jnp.where(((i >> 4) == (j >> 4)) & (tap < 3), weight, 0.0).astype(BF16)


def dot(left, right, dims=(((1,), (0,)), ((), ()))):
    return lax.dot_general(left, right, dims, preferred_element_type=F32)


def dot_left(left, weights, dims=(((1,), (0,)), ((), ()))):
    both = dot(jnp.concatenate(halves(left), 0), weights, dims)
    rows = left.shape[0]
    return both[:rows] + both[rows:]


def dot_right(weights, right, dims=(((1,), (0,)), ((), ()))):
    both = dot(weights, jnp.concatenate(halves(right), 1), dims)
    cols = right.shape[1]
    return both[:, :cols] + both[:, cols:]


def pick(shape, wanted, there):
    i = lax.broadcasted_iota(jnp.int32, shape, 0)
    j = lax.broadcasted_iota(jnp.int32, shape, 1)
    return jnp.where(wanted(i) == there(j), 1.0, 0.0).astype(BF16)


def move_bins(block, tile, source):
    move = pick((160, 256), lambda i: source * 160 + i, lambda j: tile * 160 - 3 + j)
    return dot(block[32:48, :160].astype(BF16), move)


def widen_own_kernel(place, own, out, own_cols, near_cols, far_cols):
    tile = place[1]
    cols = col_weights(tile, tile)
    out[:32, :] = dot_left(own[:32, :], cols)
    out[32:48, :] = move_bins(own, tile, tile)
    own_cols[...] = cols
    near_cols[...] = col_weights(tile, place[3])
    far_cols[...] = col_weights(tile, place[5])


def widen_kernel(place, own, near, near_cols, far, far_cols, out):
    tile = place[1]
    out[:32, :] = (
        own[:32, :]
        + dot_left(near[:32, :], near_cols[...])
        + dot_left(far[:32, :], far_cols[...])
    )
    out[32:48, :] = (
        own[32:48, :] + move_bins(near, tile, place[3]) + move_bins(far, tile, place[5])
    )


def loss_kernel(
    place,
    own,
    near,
    far,
    own_cols,
    taps,
    features_hbm,
    probe_hbm,
    loss_out,
    map_grad,
    parts,
    token_grad,
    nine,
    features,
    probe,
    sems,
):
    copies = [
        pltpu.make_async_copy(features_hbm, features, sems.at[0]),
        pltpu.make_async_copy(probe_hbm, probe, sems.at[1]),
    ]
    for copy in copies:
        copy.start()
    seq, tile = place[0], place[1]
    own_rows = row_weights(seq, seq)
    depth = jnp.zeros((32, 256), F32)
    bins = jnp.zeros((32, 256), F32)
    for block, source in ((own, seq), (near, place[2]), (far, place[4])):
        depth = depth + dot_right(row_weights(seq, source), block[:32, :])
        move = pick(
            (32, 16),
            lambda i: (i >> 4) * 1024 + seq * 8 - 3 + (i & 15),
            lambda j: (j >> 3) * 1024 + source * 8 + (j & 7),
        )
        bins = bins + dot(move, block[32:48, :].astype(BF16))
    target = (bins + 0.5) * (4.0 / NBINS) - 2.0
    error = depth - target
    loss = error * error
    for f in range(2):
        loss_out[f] = loss[f * 16 + 3 : f * 16 + 11, 3:163]
    y = lax.broadcasted_iota(jnp.int32, (32, 256), 0) & 15
    x = lax.broadcasted_iota(jnp.int32, (32, 256), 1)
    row = seq * 8 - 3 + y
    col = tile * 160 - 3 + x
    valid = (y < 14) & (x < 166) & (row >= 0) & (row < FULL_ROWS) & (col >= 0) & (col < FULL_COLS)
    grad = jnp.where(valid, 2.0 * error, 0.0)
    narrow = dot_left(dot_right(own_rows, grad, TN), own_cols[...], NT)
    for g in range(4):
        for b in range(3):
            token_grad[b * 8 : (b + 1) * 8, g * COLS : (g + 1) * COLS] = narrow[
                g * 8 : (g + 1) * 8, b * 128 : b * 128 + COLS
            ]
    grads = token_grad[...]
    map_grad[...] = lax.dot_general(
        grads, taps[...], TN, precision=PRECISE, preferred_element_type=F32
    ).astype(BF16)
    for copy in copies:
        copy.wait()
    high, low = halves(grads)
    feature_grad = jnp.dot(high, features[...], preferred_element_type=F32) + jnp.dot(
        low, features[...], preferred_element_type=F32
    )
    high, low = halves(feature_grad)
    refine = jnp.dot(high, probe[...], preferred_element_type=F32) + jnp.dot(
        low, probe[...], preferred_element_type=F32
    )
    nine[...] = jnp.zeros_like(nine)
    for b in range(3):
        nine[b * 3 : (b + 1) * 3, :P_SIZE] = refine[b * 8 : b * 8 + 3]
        nine[b * 3 : (b + 1) * 3, P_SIZE:] = feature_grad[b * 8 : b * 8 + 3]
    every = nine[:, :P_SIZE]
    for j in range(16):
        own = nine[:, P_SIZE + j * 72 : P_SIZE + (j + 1) * 72]
        parts[j] = jnp.concatenate([every, own, jnp.zeros((16, 56), F32)], 1).astype(BF16)


def plane_sum_kernel(parts, out):
    total = jnp.sum(parts[...].astype(F32), axis=0)
    every = total[:, :P_SIZE]
    for z in range(8):
        own = total[:, P_SIZE + z * 9 : P_SIZE + (z + 1) * 9]
        out[z] = jnp.concatenate([every, own, jnp.zeros((16, 119), F32)], 1).astype(BF16)


def adam_step(grad, moment, second):
    new_moment = BETA_ONE * moment + (1.0 - BETA_ONE) * grad
    new_second = BETA_TWO * second + (1.0 - BETA_TWO) * grad * grad
    return (
        new_moment
        / (1.0 - BETA_ONE**STEP)
        / (jnp.sqrt(new_second / (1.0 - BETA_TWO**STEP)) + ADAM_EPS)
    )


def step_kernel(
    parts, w_refine, mom_probe, var_probe, mom_refine, var_refine, probe_out, refine_out, taps
):
    total = jnp.sum(parts[...].astype(F32), axis=0)
    taps[...] = jnp.zeros_like(taps)
    for a in range(3):
        for b in range(3):
            i = b * 3 + a
            taps[i : i + 1] = w_refine[a, b : b + 1]
            refine_out[a, b : b + 1] = adam_step(
                total[i : i + 1, :P_SIZE], mom_refine[a, b : b + 1], var_refine[a, b : b + 1]
            )
    probe_grad = lax.dot_general(
        total[:, P_SIZE:], taps[...], TN, precision=PRECISE, preferred_element_type=F32
    )
    probe_out[...] = adam_step(probe_grad[:9], mom_probe[...], var_probe[...])


def body(
    query_act,
    key_act,
    value_act,
    residual,
    gate_scale,
    w_out,
    w_probe,
    w_refine,
    depth_bins,
    mom_probe,
    var_probe,
    mom_refine,
    var_refine,
):
    seq = lax.axis_index(SEQ)
    tile = lax.axis_index(TILE)
    odd_seq = seq & 1
    odd_tile = tile & 1
    far_seq = seq + 2 * odd_seq - 1
    far_tile = tile + 2 * odd_tile - 1
    place = jnp.stack([seq, tile, seq ^ 1, tile ^ 1, far_seq, far_tile]).astype(jnp.int32)

    taps = jnp.pad(w_refine.transpose(1, 0, 2), ((0, 0), (0, 5), (0, 0))).reshape(24, P_SIZE)
    probe, tap_weights, bins = call(
        weights_kernel,
        [
            jax.ShapeDtypeStruct((D, P_SIZE), BF16),
            jax.ShapeDtypeStruct((48, D), BF16),
            jax.ShapeDtypeStruct((16, 160), F32),
        ],
        (w_probe, taps, depth_bins.reshape(16, 160)),
        limit=16,
    )

    def split(act):
        return act.reshape(SEQ_COUNT, 1, 2, COLS * HD)

    sent = jnp.concatenate([split(query_act), split(key_act), split(value_act)], axis=1)
    here = lax.all_to_all(sent, SEQ, split_axis=0, concat_axis=0, tiled=True)
    queries = here[:, 0].reshape(ROWS, COLS * HD)
    own_kv = jnp.stack([here[:, i].reshape(ROWS, COLS * HD) for i in (1, 2)])
    swap_core = [(0, 1), (1, 0)]
    z_kv = lax.ppermute(own_kv, "z_hi", swap_core)
    core_kv = lax.ppermute(own_kv, "core", swap_core)
    query_rows, acc = attend(True, False, queries, own_kv)
    acc, probe, tap_weights, bins = lax.optimization_barrier((acc, probe, tap_weights, bins))
    acc = attend(False, False, query_rows, core_kv, acc)
    z_kv, acc = lax.optimization_barrier((z_kv, acc))
    z_core_kv = lax.ppermute(z_kv, "core", swap_core)
    acc = attend(False, False, query_rows, z_kv, acc)
    attended = attend(False, True, query_rows, z_core_kv, acc)
    merged = lax.all_to_all(
        attended.reshape(SEQ_COUNT, 2, COLS * HD), SEQ, split_axis=0, concat_axis=0, tiled=True
    ).reshape(ROWS, COLS * HD)

    features, tap_maps = call(
        features_kernel,
        [jax.ShapeDtypeStruct((160, D), BF16), jax.ShapeDtypeStruct((48, 384), F32)],
        (
            merged,
            residual.reshape(160, D),
            gate_scale.reshape(1, D),
            w_out,
            tap_weights,
            bins,
        ),
        [pltpu.VMEM((TOKENS, 128), F32), pltpu.VMEM((160, D), F32)],
        limit=32,
    )
    tile_far = [(1, 2), (2, 1)]
    seq_near = [(i, i ^ 1) for i in range(SEQ_COUNT)]
    seq_far = [(i, i + 2 * (i & 1) - 1) for i in range(1, SEQ_COUNT - 1)]
    map_far = lax.ppermute(tap_maps, TILE, tile_far)
    map_near = lax.ppermute(tap_maps, "core", swap_core)
    cols = jax.ShapeDtypeStruct((384, 256), BF16)
    wide, own_cols, near_cols, far_cols = call(
        widen_own_kernel,
        [jax.ShapeDtypeStruct((48, 256), F32), cols, cols, cols],
        (place, tap_maps),
        limit=16,
    )
    wide = call(
        widen_kernel,
        jax.ShapeDtypeStruct((48, 256), F32),
        (place, wide, map_near, near_cols, map_far, far_cols),
        limit=16,
    )
    wide_far = lax.ppermute(wide, SEQ, seq_far)
    wide_near = lax.ppermute(wide, SEQ, seq_near)
    loss_map, map_grad, parts = call(
        loss_kernel,
        [
            jax.ShapeDtypeStruct((2, 8, 160), F32),
            jax.ShapeDtypeStruct((160, P_SIZE), BF16),
            jax.ShapeDtypeStruct((16, 16, 384), BF16),
        ],
        (place, wide, wide_near, wide_far, own_cols, taps, features, probe),
        [
            pltpu.VMEM((24, 160), F32),
            pltpu.VMEM((16, P_SIZE + D), F32),
            pltpu.VMEM((160, D), BF16),
            pltpu.VMEM((D, P_SIZE), BF16),
            pltpu.SemaphoreType.DMA((2,)),
        ],
        limit=16,
        left=2,
    )
    parts = lax.all_to_all(parts, PLANE, split_axis=0, concat_axis=0, tiled=True)
    parts = call(plane_sum_kernel, jax.ShapeDtypeStruct((8, 16, 384), BF16), (parts,), limit=16)
    parts = lax.all_to_all(parts, COLUMN, split_axis=0, concat_axis=0, tiled=True)
    probe_step, refine_step = call(
        step_kernel,
        [
            jax.ShapeDtypeStruct((9, P_SIZE), F32),
            jax.ShapeDtypeStruct((3, 3, P_SIZE), F32),
        ],
        (parts, w_refine, mom_probe, var_probe, mom_refine, var_refine),
        [pltpu.VMEM((16, P_SIZE), F32)],
        limit=16,
    )
    return (loss_map, map_grad.reshape(2, 2, COLS, P_SIZE), probe_step, refine_step)


def solution(mesh):
    fine = Mesh(mesh.devices.reshape(4, 4, 2, 2, 2), ("y", "x", "z_lo", "z_hi", "core"))
    slab = (*SEQ, *TILE)
    in_specs = (
        P(None, None, SEQ, TILE),
        P(None, None, SEQ, TILE),
        P(None, None, SEQ, TILE),
        P(None, SEQ, TILE, None),
        P(),
        P(),
        P(),
        P(),
        P(None, SEQ, TILE),
        P(slab, None),
        P(slab, None),
        P(),
        P(),
    )
    out_specs = (
        P(None, SEQ, TILE),
        P(None, SEQ, TILE, None),
        P(slab, None),
        P(),
    )
    return jax.shard_map(body, mesh=fine, in_specs=in_specs, out_specs=out_specs, check_vma=False)
```

```python
import functools
import math

import jax
import jax.numpy as jnp
from jax import lax
from jax.experimental import pallas as pl
from jax.experimental.pallas import tpu as pltpu
from jax.sharding import Mesh, PartitionSpec as P

HD = 72
HEADS = 16
D = 1152
P_SIZE = 256
NBINS = 256
STEP = 10
ROWS = 64
COLS = 40
TOKENS = ROWS * COLS
BLOCK = 512
SEQ_COUNT = 32
TILE_COUNT = 4
FULL_ROWS = 256
FULL_COLS = 640

BETA_ONE = 0.9
BETA_TWO = 0.999
ADAM_EPS = 1e-08
NORM_EPS = 1e-06
PRECISE = lax.Precision.HIGHEST
EXP_SCALE = HD ** (-0.5) * math.log2(math.e)

SEQ = ("y", "x", "z_lo")
TILE = ("z_hi", "core")
PLANE = ("y", "x")
COLUMN = ("z_lo", "z_hi", "core")

NT = (((1,), (1,)), ((), ()))
TN = (((0,), (0,)), ((), ()))
F32 = jnp.float32
BF16 = jnp.bfloat16
VMEM = pl.BlockSpec(memory_space=pltpu.VMEM)
SMEM = pl.BlockSpec(memory_space=pltpu.SMEM)
HBM = pl.BlockSpec(memory_space=pltpu.HBM)


def call(
    kernel,
    out_shape,
    operands,
    scratch=(),
    flops=0,
    bytes_accessed=0,
    transcendentals=0,
    limit=56,
    left=(),
    left_out=(),
):
    in_specs = [SMEM if x.dtype == jnp.int32 and x.ndim == 1 else VMEM for x in operands]
    for i in left:
        in_specs[i] = HBM
    many = isinstance(out_shape, (list, tuple))
    return pl.pallas_call(
        kernel,
        out_shape=out_shape,
        in_specs=in_specs,
        out_specs=[HBM if i in left_out else VMEM for i in range(len(out_shape))] if many else VMEM,
        scratch_shapes=list(scratch),
        compiler_params=pltpu.CompilerParams(vmem_limit_bytes=limit * 2**20),
        cost_estimate=pl.CostEstimate(
            flops=flops, bytes_accessed=bytes_accessed, transcendentals=transcendentals
        ),
    )(*operands)


def halves(value):
    high = value.astype(BF16)
    low = (value - high.astype(F32)).astype(BF16)
    return high, low


def unpack(packed, rows):
    for c in range(COLS):
        rows[c * ROWS : (c + 1) * ROWS, :HD] = packed[:, c * HD : (c + 1) * HD]


def attend_kernel(first, last, unrolled, *refs):
    if first:
        q_ref, kv_ref, query_rows, acc_out, key_rows, value_rows, scores_ref = refs
        query_rows[...] = jnp.zeros_like(query_rows)
        unpack(q_ref, query_rows)
    elif last:
        query_rows, kv_ref, acc_ref, out_ref, key_rows, value_rows, scores_ref, acc_out = refs
    else:
        query_rows, kv_ref, acc_ref, acc_out, key_rows, value_rows, scores_ref = refs
    key_rows[...] = jnp.zeros_like(key_rows)
    lane = lax.broadcasted_iota(jnp.int32, (TOKENS, 128), 1)
    value_rows[...] = jnp.where(lane == HD, 1.0, 0.0).astype(BF16)
    unpack(kv_ref.at[0], key_rows)
    unpack(kv_ref.at[1], value_rows)

    def scores(low, slot):
        scores_ref[slot] = lax.dot_general(
            query_rows[pl.ds(low, BLOCK), :], key_rows[...], NT, preferred_element_type=F32
        )

    def finish(low, slot):
        rows = pl.ds(low, BLOCK)
        block = scores_ref[slot]
        top = jnp.max(block, axis=1, keepdims=True)
        if not first:
            old = acc_ref[rows, :]
            old_top = old[:, HD + 1 : HD + 2]
            top = jnp.maximum(top, old_top)
        weights = jnp.exp2((block - top) * EXP_SCALE).astype(BF16)
        total = jnp.dot(weights, value_rows[...], preferred_element_type=F32)
        if not first:
            total = total + old * jnp.exp2((old_top - top) * EXP_SCALE)
        if last:
            acc_out[rows, :] = total / total[:, HD : HD + 1]
        else:
            lane = lax.broadcasted_iota(jnp.int32, (BLOCK, 128), 1)
            acc_out[rows, :] = jnp.where(lane == HD + 1, top, total)

    def pair(j, carry):
        low = j * 2 * BLOCK if isinstance(j, int) else pl.multiple_of(j * 2 * BLOCK, BLOCK)
        scores(low + BLOCK, 1)
        finish(low, 0)
        scores(low + 2 * BLOCK, 0)
        finish(low + BLOCK, 1)
        return carry

    scores(0, 0)
    if unrolled:
        pair(0, 0)
        pair(1, 0)
    else:
        lax.fori_loop(0, 2, pair, 0)
    finish(TOKENS - BLOCK, 0)
    if last:
        for c in range(COLS):
            out_ref[:, c * HD : (c + 1) * HD] = acc_out[c * ROWS : (c + 1) * ROWS, :HD].astype(BF16)


def attend(first, last, *operands, unrolled=True):
    rows = jax.ShapeDtypeStruct((TOKENS, 128), BF16)
    acc = jax.ShapeDtypeStruct((TOKENS, 128), F32)
    if first:
        out = [rows, acc]
    elif last:
        out = jax.ShapeDtypeStruct((ROWS, COLS * HD), BF16)
    else:
        out = acc
    scratch = [
        pltpu.VMEM((TOKENS, 128), BF16),
        pltpu.VMEM((TOKENS, 128), BF16),
        pltpu.VMEM((2, BLOCK, TOKENS), F32),
    ]
    if last:
        scratch.append(pltpu.VMEM((TOKENS, 128), F32))
    return call(
        functools.partial(attend_kernel, first, last, unrolled),
        out,
        operands,
        scratch,
        flops=4 * TOKENS * TOKENS * 256,
        bytes_accessed=4 * 2**20,
        transcendentals=TOKENS * TOKENS,
        limit=24,
    )


def weights_kernel(w_probe, taps, tap_weights):
    probe = w_probe[...].astype(BF16)
    high, low = halves(taps[...])
    rest = (taps[...] - high.astype(F32) - low.astype(F32)).astype(BF16)
    folded = lax.dot_general(
        jnp.concatenate([high, low, rest], 0).astype(BF16), probe, NT, preferred_element_type=F32
    )
    folded = folded[:24] + folded[24:48] + folded[48:72]
    tap_high, tap_low = halves(folded)
    tap_weights[...] = jnp.concatenate([tap_high.astype(F32), tap_low.astype(F32)], 0).astype(BF16)


def features_kernel(
    merged,
    residual,
    gate,
    w_out,
    tap_weights,
    bins_hbm,
    features_hbm,
    tap_maps,
    spread,
    joined,
    bins,
    features_ref,
    sems,
):
    bins_copy = pltpu.make_async_copy(bins_hbm, bins, sems.at[0])
    bins_copy.start()
    for c in range(COLS):
        spread[c * ROWS : (c + 1) * ROWS, :HD] = merged[:, c * HD : (c + 1) * HD].astype(F32)
    for h in range(HEADS):
        for g in range(4):
            f, r = divmod(g, 2)
            piece = spread[pl.ds(f * 2 * HEADS + h * 2 + r, COLS, stride=ROWS), :]
            joined[g * COLS : (g + 1) * COLS, h * HD : (h + 1) * HD] = piece[:, :HD]
    mixed = jnp.dot(joined[...].astype(BF16), w_out[...], preferred_element_type=F32)
    stream = residual[...].astype(F32) + gate[...] * mixed
    centered = stream - jnp.mean(stream, axis=1, keepdims=True)
    var = jnp.mean(centered * centered, axis=1, keepdims=True)
    features = (centered * lax.rsqrt(var + NORM_EPS)).astype(BF16)
    features_ref[...] = features
    features_copy = pltpu.make_async_copy(features_ref, features_hbm, sems.at[1])
    features_copy.start()
    maps = lax.dot_general(tap_weights[...], features, NT, preferred_element_type=F32)
    maps = maps[:24] + maps[24:48]
    tap_maps[...] = jnp.zeros_like(tap_maps)
    for g in range(4):
        for b in range(3):
            tap_maps[g * 8 : (g + 1) * 8, b * 128 : b * 128 + COLS] = maps[
                b * 8 : (b + 1) * 8, g * COLS : (g + 1) * COLS
            ]
    bins_copy.wait()
    tap_maps[32:48, :160] = bins[...].astype(F32)
    features_copy.wait()


def hat(offset):
    return jnp.maximum(0.0, 1.0 - jnp.abs(offset))


def interp(pixel, latent, count_in):
    source = (pixel.astype(F32) + 0.5) * 0.25 - 0.5
    offset = source - latent.astype(F32)
    weight = hat(offset)
    weight = weight + jnp.where(latent == 0, hat(offset + 1.0), 0.0)
    weight = weight + jnp.where(latent == count_in - 1, hat(offset - 1.0), 0.0)
    inside = (pixel >= 0) & (pixel < 4 * count_in) & (latent >= 0) & (latent < count_in)
    return jnp.where(inside, weight, 0.0)


def col_weights(tile, source):
    shape = (384, 256)
    i = lax.broadcasted_iota(jnp.int32, shape, 0)
    x = lax.broadcasted_iota(jnp.int32, shape, 1)
    tap = i >> 7
    c = i & 127
    weight = interp(tile * 160 - 4 + x + tap, source * COLS + c, TILE_COUNT * COLS)
    return jnp.where(c < COLS, weight, 0.0).astype(BF16)


def row_weights(seq, source):
    shape = (32, 32)
    i = lax.broadcasted_iota(jnp.int32, shape, 0)
    j = lax.broadcasted_iota(jnp.int32, shape, 1)
    y = i & 15
    tap = j & 7
    weight = interp(seq * 8 - 4 + y + tap, source * 2 + ((j >> 3) & 1), ROWS)
    return jnp.where(((i >> 4) == (j >> 4)) & (tap < 3), weight, 0.0).astype(BF16)


def dot(left, right, dims=(((1,), (0,)), ((), ()))):
    return lax.dot_general(left, right, dims, preferred_element_type=F32)


def dot_left(left, weights, dims=(((1,), (0,)), ((), ()))):
    both = dot(jnp.concatenate(halves(left), 0), weights, dims)
    rows = left.shape[0]
    return both[:rows] + both[rows:]


def dot_right(weights, right, dims=(((1,), (0,)), ((), ()))):
    both = dot(weights, jnp.concatenate(halves(right), 1), dims)
    cols = right.shape[1]
    return both[:, :cols] + both[:, cols:]


def pick(shape, wanted, there):
    i = lax.broadcasted_iota(jnp.int32, shape, 0)
    j = lax.broadcasted_iota(jnp.int32, shape, 1)
    return jnp.where(wanted(i) == there(j), 1.0, 0.0).astype(BF16)


def move_bins(block, tile, source):
    move = pick((160, 256), lambda i: source * 160 + i, lambda j: tile * 160 - 3 + j)
    return dot(block[32:48, :160].astype(BF16), move)


def widen_own_kernel(place, own, out, own_cols, near_cols, far_cols):
    tile = place[1]
    cols = col_weights(tile, tile)
    out[:32, :] = dot_left(own[:32, :], cols)
    out[32:48, :] = move_bins(own, tile, tile)
    own_cols[...] = cols
    near_cols[...] = col_weights(tile, place[3])
    far_cols[...] = col_weights(tile, place[5])


def widen_kernel(place, own, near, near_cols, far, far_cols, out):
    tile = place[1]
    out[:32, :] = (
        own[:32, :]
        + dot_left(near[:32, :], near_cols[...])
        + dot_left(far[:32, :], far_cols[...])
    )
    out[32:48, :] = (
        own[32:48, :] + move_bins(near, tile, place[3]) + move_bins(far, tile, place[5])
    )


def loss_kernel(
    place,
    own,
    near,
    far,
    own_cols,
    taps,
    features_hbm,
    w_probe_hbm,
    loss_out,
    map_grad,
    parts,
    token_grad,
    nine,
    features,
    w_probe,
    sems,
):
    copies = [
        pltpu.make_async_copy(features_hbm, features, sems.at[0]),
        pltpu.make_async_copy(w_probe_hbm, w_probe, sems.at[1]),
    ]
    for copy in copies:
        copy.start()
    seq, tile = place[0], place[1]
    own_rows = row_weights(seq, seq)
    depth = jnp.zeros((32, 256), F32)
    bins = jnp.zeros((32, 256), F32)
    for block, source in ((own, seq), (near, place[2]), (far, place[4])):
        depth = depth + dot_right(row_weights(seq, source), block[:32, :])
        move = pick(
            (32, 16),
            lambda i: (i >> 4) * 1024 + seq * 8 - 3 + (i & 15),
            lambda j: (j >> 3) * 1024 + source * 8 + (j & 7),
        )
        bins = bins + dot(move, block[32:48, :].astype(BF16))
    target = (bins + 0.5) * (4.0 / NBINS) - 2.0
    error = depth - target
    loss = error * error
    for f in range(2):
        loss_out[f] = loss[f * 16 + 3 : f * 16 + 11, 3:163]
    y = lax.broadcasted_iota(jnp.int32, (32, 256), 0) & 15
    x = lax.broadcasted_iota(jnp.int32, (32, 256), 1)
    row = seq * 8 - 3 + y
    col = tile * 160 - 3 + x
    valid = (y < 14) & (x < 166) & (row >= 0) & (row < FULL_ROWS) & (col >= 0) & (col < FULL_COLS)
    grad = jnp.where(valid, 2.0 * error, 0.0)
    narrow = dot_left(dot_right(own_rows, grad, TN), own_cols[...], NT)
    for g in range(4):
        for b in range(3):
            token_grad[b * 8 : (b + 1) * 8, g * COLS : (g + 1) * COLS] = narrow[
                g * 8 : (g + 1) * 8, b * 128 : b * 128 + COLS
            ]
    grads = token_grad[...]
    map_grad[...] = lax.dot_general(
        grads, taps[...], TN, precision=PRECISE, preferred_element_type=F32
    ).astype(BF16)
    for copy in copies:
        copy.wait()
    high, low = halves(grads)
    feature_grad = jnp.dot(high, features[...], preferred_element_type=F32) + jnp.dot(
        low, features[...], preferred_element_type=F32
    )
    high, low = halves(feature_grad)
    probe = w_probe[...].astype(BF16)
    refine = dot(high, probe) + dot(low, probe)
    nine[...] = jnp.zeros_like(nine)
    for b in range(3):
        nine[b * 3 : (b + 1) * 3, :P_SIZE] = refine[b * 8 : b * 8 + 3]
        nine[b * 3 : (b + 1) * 3, P_SIZE:] = feature_grad[b * 8 : b * 8 + 3]
    every = nine[:, :P_SIZE]
    for j in range(16):
        own = nine[:, P_SIZE + j * 72 : P_SIZE + (j + 1) * 72]
        parts[j] = jnp.concatenate([every, own, jnp.zeros((16, 56), F32)], 1).astype(BF16)


def plane_sum_kernel(parts, out):
    total = jnp.sum(parts[...].astype(F32), axis=0)
    every = total[:, :P_SIZE]
    for z in range(8):
        own = total[:, P_SIZE + z * 9 : P_SIZE + (z + 1) * 9]
        out[z] = jnp.concatenate([every, own, jnp.zeros((16, 119), F32)], 1).astype(BF16)


def adam_step(grad, moment, second):
    new_moment = BETA_ONE * moment + (1.0 - BETA_ONE) * grad
    new_second = BETA_TWO * second + (1.0 - BETA_TWO) * grad * grad
    return (
        new_moment
        / (1.0 - BETA_ONE**STEP)
        / (jnp.sqrt(new_second / (1.0 - BETA_TWO**STEP)) + ADAM_EPS)
    )


def step_kernel(
    parts, w_refine, mom_probe, var_probe, mom_refine, var_refine, probe_out, refine_out, taps
):
    total = jnp.sum(parts[...].astype(F32), axis=0)
    taps[...] = jnp.zeros_like(taps)
    for a in range(3):
        for b in range(3):
            i = b * 3 + a
            taps[i : i + 1] = w_refine[a, b : b + 1]
            refine_out[a, b : b + 1] = adam_step(
                total[i : i + 1, :P_SIZE], mom_refine[a, b : b + 1], var_refine[a, b : b + 1]
            )
    probe_grad = lax.dot_general(
        total[:, P_SIZE:], taps[...], TN, precision=PRECISE, preferred_element_type=F32
    )
    probe_out[...] = adam_step(probe_grad[:9], mom_probe[...], var_probe[...])


def body(
    query_act,
    key_act,
    value_act,
    residual,
    gate_scale,
    w_out,
    w_probe,
    w_refine,
    depth_bins,
    mom_probe,
    var_probe,
    mom_refine,
    var_refine,
):
    seq = lax.axis_index(SEQ)
    tile = lax.axis_index(TILE)
    odd_seq = seq & 1
    odd_tile = tile & 1
    far_seq = seq + 2 * odd_seq - 1
    far_tile = tile + 2 * odd_tile - 1
    place = jnp.stack([seq, tile, seq ^ 1, tile ^ 1, far_seq, far_tile]).astype(jnp.int32)

    taps = jnp.pad(w_refine.transpose(1, 0, 2), ((0, 0), (0, 5), (0, 0))).reshape(24, P_SIZE)
    def split(act):
        return act.reshape(SEQ_COUNT, 1, 2, COLS * HD)

    sent = jnp.concatenate([split(query_act), split(key_act), split(value_act)], axis=1)
    here = lax.all_to_all(sent, SEQ, split_axis=0, concat_axis=0, tiled=True)
    queries = here[:, 0].reshape(ROWS, COLS * HD)
    own_kv = jnp.stack([here[:, i].reshape(ROWS, COLS * HD) for i in (1, 2)])
    swap_core = [(0, 1), (1, 0)]
    z_kv = lax.ppermute(own_kv, "z_hi", swap_core)
    core_kv = lax.ppermute(own_kv, "core", swap_core)
    query_rows, acc = attend(True, False, queries, own_kv)
    acc = attend(False, False, query_rows, core_kv, acc, unrolled=False)
    z_kv, acc = lax.optimization_barrier((z_kv, acc))
    z_core_kv = lax.ppermute(z_kv, "core", swap_core)
    acc = attend(False, False, query_rows, z_kv, acc, unrolled=False)
    attended = attend(False, True, query_rows, z_core_kv, acc)
    attended, w_probe_later = lax.optimization_barrier((attended, w_probe))
    tap_weights = call(
        weights_kernel,
        jax.ShapeDtypeStruct((48, D), BF16),
        (w_probe_later, taps),
        flops=2 * 72 * P_SIZE * D,
        bytes_accessed=4 * P_SIZE * D,
        limit=16,
    )
    merged = lax.all_to_all(
        attended.reshape(SEQ_COUNT, 2, COLS * HD), SEQ, split_axis=0, concat_axis=0, tiled=True
    ).reshape(ROWS, COLS * HD)

    features, tap_maps = call(
        features_kernel,
        [jax.ShapeDtypeStruct((160, D), BF16), jax.ShapeDtypeStruct((48, 384), F32)],
        (
            merged,
            residual.reshape(160, D),
            gate_scale.reshape(1, D),
            w_out,
            tap_weights,
            depth_bins.reshape(16, 160),
        ),
        [
            pltpu.VMEM((TOKENS, 128), F32),
            pltpu.VMEM((160, D), F32),
            pltpu.VMEM((16, 160), jnp.int32),
            pltpu.VMEM((160, D), BF16),
            pltpu.SemaphoreType.DMA((2,)),
        ],
        limit=24,
        left=(5,),
        left_out=(0,),
    )
    tile_far = [(1, 2), (2, 1)]
    seq_near = [(i, i ^ 1) for i in range(SEQ_COUNT)]
    seq_far = [(i, i + 2 * (i & 1) - 1) for i in range(1, SEQ_COUNT - 1)]
    map_far = lax.ppermute(tap_maps, TILE, tile_far)
    map_near = lax.ppermute(tap_maps, "core", swap_core)
    cols = jax.ShapeDtypeStruct((384, 256), BF16)
    wide, own_cols, near_cols, far_cols = call(
        widen_own_kernel,
        [jax.ShapeDtypeStruct((48, 256), F32), cols, cols, cols],
        (place, tap_maps),
        limit=16,
    )
    wide = call(
        widen_kernel,
        jax.ShapeDtypeStruct((48, 256), F32),
        (place, wide, map_near, near_cols, map_far, far_cols),
        limit=16,
    )
    wide_far = lax.ppermute(wide, SEQ, seq_far)
    wide_near = lax.ppermute(wide, SEQ, seq_near)
    loss_map, map_grad, parts = call(
        loss_kernel,
        [
            jax.ShapeDtypeStruct((2, 8, 160), F32),
            jax.ShapeDtypeStruct((160, P_SIZE), BF16),
            jax.ShapeDtypeStruct((16, 16, 384), BF16),
        ],
        (place, wide, wide_near, wide_far, own_cols, taps, features, w_probe),
        [
            pltpu.VMEM((24, 160), F32),
            pltpu.VMEM((16, P_SIZE + D), F32),
            pltpu.VMEM((160, D), BF16),
            pltpu.VMEM((D, P_SIZE), F32),
            pltpu.SemaphoreType.DMA((2,)),
        ],
        limit=16,
        left=(6, 7),
    )
    parts = lax.all_to_all(parts, PLANE, split_axis=0, concat_axis=0, tiled=True)
    parts = call(plane_sum_kernel, jax.ShapeDtypeStruct((8, 16, 384), BF16), (parts,), limit=16)
    parts = lax.all_to_all(parts, COLUMN, split_axis=0, concat_axis=0, tiled=True)
    probe_step, refine_step = call(
        step_kernel,
        [
            jax.ShapeDtypeStruct((9, P_SIZE), F32),
            jax.ShapeDtypeStruct((3, 3, P_SIZE), F32),
        ],
        (parts, w_refine, mom_probe, var_probe, mom_refine, var_refine),
        [pltpu.VMEM((16, P_SIZE), F32)],
        limit=16,
    )
    return (loss_map, map_grad.reshape(2, 2, COLS, P_SIZE), probe_step, refine_step)


def solution(mesh):
    fine = Mesh(mesh.devices.reshape(4, 4, 2, 2, 2), ("y", "x", "z_lo", "z_hi", "core"))
    slab = (*SEQ, *TILE)
    in_specs = (
        P(None, None, SEQ, TILE),
        P(None, None, SEQ, TILE),
        P(None, None, SEQ, TILE),
        P(None, SEQ, TILE, None),
        P(),
        P(),
        P(),
        P(),
        P(None, SEQ, TILE),
        P(slab, None),
        P(slab, None),
        P(),
        P(),
    )
    out_specs = (
        P(None, SEQ, TILE),
        P(None, SEQ, TILE, None),
        P(slab, None),
        P(),
    )
    return jax.shard_map(body, mesh=fine, in_specs=in_specs, out_specs=out_specs, check_vma=False)
```

```python
import functools
import math

import jax
import jax.numpy as jnp
from jax import lax
from jax.experimental import pallas as pl
from jax.experimental.pallas import tpu as pltpu
from jax.sharding import Mesh, PartitionSpec as P

HD = 72
HEADS = 16
D = 1152
P_SIZE = 256
NBINS = 256
STEP = 10
ROWS = 64
COLS = 40
TOKENS = ROWS * COLS
BLOCK = 512
SEQ_COUNT = 32
TILE_COUNT = 4
FULL_ROWS = 256
FULL_COLS = 640

BETA_ONE = 0.9
BETA_TWO = 0.999
ADAM_EPS = 1e-08
NORM_EPS = 1e-06
PRECISE = lax.Precision.HIGHEST
EXP_SCALE = HD ** (-0.5) * math.log2(math.e)

SEQ = ("y", "x", "z_lo")
TILE = ("z_hi", "core")
PLANE = ("y", "x")
COLUMN = ("z_lo", "z_hi", "core")

NT = (((1,), (1,)), ((), ()))
TN = (((0,), (0,)), ((), ()))
F32 = jnp.float32
BF16 = jnp.bfloat16
VMEM = pl.BlockSpec(memory_space=pltpu.VMEM)
SMEM = pl.BlockSpec(memory_space=pltpu.SMEM)
HBM = pl.BlockSpec(memory_space=pltpu.HBM)


def call(
    kernel,
    out_shape,
    operands,
    scratch=(),
    flops=0,
    bytes_accessed=0,
    transcendentals=0,
    limit=56,
    left=(),
    left_out=(),
):
    in_specs = [SMEM if x.dtype == jnp.int32 and x.ndim == 1 else VMEM for x in operands]
    for i in left:
        in_specs[i] = HBM
    many = isinstance(out_shape, (list, tuple))
    return pl.pallas_call(
        kernel,
        out_shape=out_shape,
        in_specs=in_specs,
        out_specs=[HBM if i in left_out else VMEM for i in range(len(out_shape))] if many else VMEM,
        scratch_shapes=list(scratch),
        compiler_params=pltpu.CompilerParams(vmem_limit_bytes=limit * 2**20),
        cost_estimate=pl.CostEstimate(
            flops=flops, bytes_accessed=bytes_accessed, transcendentals=transcendentals
        ),
    )(*operands)


def halves(value):
    high = value.astype(BF16)
    low = (value - high.astype(F32)).astype(BF16)
    return high, low


def unpack(packed, rows):
    for c in range(COLS):
        rows[c * ROWS : (c + 1) * ROWS, :HD] = packed[:, c * HD : (c + 1) * HD]


def attend_kernel(first, last, unrolled, *refs):
    if first:
        q_ref, kv_ref, query_rows, acc_out, key_rows, value_rows, scores_ref = refs
        query_rows[...] = jnp.zeros_like(query_rows)
        unpack(q_ref, query_rows)
    elif last:
        query_rows, kv_ref, acc_ref, out_ref, key_rows, value_rows, scores_ref, acc_out = refs
    else:
        query_rows, kv_ref, acc_ref, acc_out, key_rows, value_rows, scores_ref = refs
    key_rows[...] = jnp.zeros_like(key_rows)
    lane = lax.broadcasted_iota(jnp.int32, (TOKENS, 128), 1)
    value_rows[...] = jnp.where(lane == HD, 1.0, 0.0).astype(BF16)
    unpack(kv_ref.at[0], key_rows)
    unpack(kv_ref.at[1], value_rows)

    def scores(low, slot):
        scores_ref[slot] = lax.dot_general(
            query_rows[pl.ds(low, BLOCK), :], key_rows[...], NT, preferred_element_type=F32
        )

    def finish(low, slot):
        rows = pl.ds(low, BLOCK)
        block = scores_ref[slot]
        top = jnp.max(block, axis=1, keepdims=True)
        if not first:
            old = acc_ref[rows, :]
            old_top = old[:, HD + 1 : HD + 2]
            top = jnp.maximum(top, old_top)
        weights = jnp.exp2((block - top) * EXP_SCALE).astype(BF16)
        total = jnp.dot(weights, value_rows[...], preferred_element_type=F32)
        if not first:
            total = total + old * jnp.exp2((old_top - top) * EXP_SCALE)
        if last:
            acc_out[rows, :] = total / total[:, HD : HD + 1]
        else:
            lane = lax.broadcasted_iota(jnp.int32, (BLOCK, 128), 1)
            acc_out[rows, :] = jnp.where(lane == HD + 1, top, total)

    def pair(j, carry):
        low = j * 2 * BLOCK if isinstance(j, int) else pl.multiple_of(j * 2 * BLOCK, BLOCK)
        scores(low + BLOCK, 1)
        finish(low, 0)
        scores(low + 2 * BLOCK, 0)
        finish(low + BLOCK, 1)
        return carry

    scores(0, 0)
    if unrolled:
        pair(0, 0)
        pair(1, 0)
    else:
        lax.fori_loop(0, 2, pair, 0)
    finish(TOKENS - BLOCK, 0)
    if last:
        for c in range(COLS):
            out_ref[:, c * HD : (c + 1) * HD] = acc_out[c * ROWS : (c + 1) * ROWS, :HD].astype(BF16)


def attend(first, last, *operands, unrolled=True):
    rows = jax.ShapeDtypeStruct((TOKENS, 128), BF16)
    acc = jax.ShapeDtypeStruct((TOKENS, 128), F32)
    if first:
        out = [rows, acc]
    elif last:
        out = jax.ShapeDtypeStruct((ROWS, COLS * HD), BF16)
    else:
        out = acc
    scratch = [
        pltpu.VMEM((TOKENS, 128), BF16),
        pltpu.VMEM((TOKENS, 128), BF16),
        pltpu.VMEM((2, BLOCK, TOKENS), F32),
    ]
    if last:
        scratch.append(pltpu.VMEM((TOKENS, 128), F32))
    return call(
        functools.partial(attend_kernel, first, last, unrolled),
        out,
        operands,
        scratch,
        flops=4 * TOKENS * TOKENS * 256,
        bytes_accessed=4 * 2**20,
        transcendentals=TOKENS * TOKENS,
        limit=24,
    )


def weights_kernel(w_probe, taps, tap_weights):
    probe = w_probe[...].astype(BF16)
    high, low = halves(taps[...])
    rest = (taps[...] - high.astype(F32) - low.astype(F32)).astype(BF16)
    folded = lax.dot_general(
        jnp.concatenate([high, low, rest], 0).astype(BF16), probe, NT, preferred_element_type=F32
    )
    folded = folded[:24] + folded[24:48] + folded[48:72]
    tap_high, tap_low = halves(folded)
    tap_weights[...] = jnp.concatenate([tap_high.astype(F32), tap_low.astype(F32)], 0).astype(BF16)


def features_kernel(
    merged,
    residual,
    gate,
    w_out,
    tap_weights,
    bins_hbm,
    features_hbm,
    tap_maps,
    spread,
    joined,
    bins,
    features_ref,
    sems,
):
    bins_copy = pltpu.make_async_copy(bins_hbm, bins, sems.at[0])
    bins_copy.start()
    for c in range(COLS):
        spread[c * ROWS : (c + 1) * ROWS, :HD] = merged[:, c * HD : (c + 1) * HD].astype(F32)
    for h in range(HEADS):
        for g in range(4):
            f, r = divmod(g, 2)
            piece = spread[pl.ds(f * 2 * HEADS + h * 2 + r, COLS, stride=ROWS), :]
            joined[g * COLS : (g + 1) * COLS, h * HD : (h + 1) * HD] = piece[:, :HD]
    mixed = jnp.dot(joined[...].astype(BF16), w_out[...], preferred_element_type=F32)
    stream = residual[...].astype(F32) + gate[...] * mixed
    centered = stream - jnp.mean(stream, axis=1, keepdims=True)
    var = jnp.mean(centered * centered, axis=1, keepdims=True)
    features = (centered * lax.rsqrt(var + NORM_EPS)).astype(BF16)
    features_ref[...] = features
    features_copy = pltpu.make_async_copy(features_ref, features_hbm, sems.at[1])
    features_copy.start()
    maps = lax.dot_general(tap_weights[...], features, NT, preferred_element_type=F32)
    maps = maps[:24] + maps[24:48]
    tap_maps[...] = jnp.zeros_like(tap_maps)
    for g in range(4):
        for b in range(3):
            tap_maps[g * 8 : (g + 1) * 8, b * 128 : b * 128 + COLS] = maps[
                b * 8 : (b + 1) * 8, g * COLS : (g + 1) * COLS
            ]
    bins_copy.wait()
    tap_maps[32:48, :160] = bins[...].astype(F32)
    features_copy.wait()


def hat(offset):
    return jnp.maximum(0.0, 1.0 - jnp.abs(offset))


def interp(pixel, latent, count_in):
    source = (pixel.astype(F32) + 0.5) * 0.25 - 0.5
    offset = source - latent.astype(F32)
    weight = hat(offset)
    weight = weight + jnp.where(latent == 0, hat(offset + 1.0), 0.0)
    weight = weight + jnp.where(latent == count_in - 1, hat(offset - 1.0), 0.0)
    inside = (pixel >= 0) & (pixel < 4 * count_in) & (latent >= 0) & (latent < count_in)
    return jnp.where(inside, weight, 0.0)


def col_weights(tile, source):
    shape = (384, 256)
    i = lax.broadcasted_iota(jnp.int32, shape, 0)
    x = lax.broadcasted_iota(jnp.int32, shape, 1)
    tap = i >> 7
    c = i & 127
    weight = interp(tile * 160 - 4 + x + tap, source * COLS + c, TILE_COUNT * COLS)
    return jnp.where(c < COLS, weight, 0.0).astype(BF16)


def row_weights(seq, source):
    shape = (32, 32)
    i = lax.broadcasted_iota(jnp.int32, shape, 0)
    j = lax.broadcasted_iota(jnp.int32, shape, 1)
    y = i & 15
    tap = j & 7
    weight = interp(seq * 8 - 4 + y + tap, source * 2 + ((j >> 3) & 1), ROWS)
    return jnp.where(((i >> 4) == (j >> 4)) & (tap < 3), weight, 0.0).astype(BF16)


def dot(left, right, dims=(((1,), (0,)), ((), ()))):
    return lax.dot_general(left, right, dims, preferred_element_type=F32)


def dot_left(left, weights, dims=(((1,), (0,)), ((), ()))):
    both = dot(jnp.concatenate(halves(left), 0), weights, dims)
    rows = left.shape[0]
    return both[:rows] + both[rows:]


def dot_right(weights, right, dims=(((1,), (0,)), ((), ()))):
    both = dot(weights, jnp.concatenate(halves(right), 1), dims)
    cols = right.shape[1]
    return both[:, :cols] + both[:, cols:]


def pick(shape, wanted, there):
    i = lax.broadcasted_iota(jnp.int32, shape, 0)
    j = lax.broadcasted_iota(jnp.int32, shape, 1)
    return jnp.where(wanted(i) == there(j), 1.0, 0.0).astype(BF16)


def move_bins(block, tile, source):
    move = pick((160, 256), lambda i: source * 160 + i, lambda j: tile * 160 - 3 + j)
    return dot(block[32:48, :160].astype(BF16), move)


def widen_own_kernel(place, own, out, own_cols, near_cols, far_cols):
    tile = place[1]
    cols = col_weights(tile, tile)
    out[:32, :] = dot_left(own[:32, :], cols)
    out[32:48, :] = move_bins(own, tile, tile)
    own_cols[...] = cols
    near_cols[...] = col_weights(tile, place[3])
    far_cols[...] = col_weights(tile, place[5])


def widen_kernel(place, own, near, near_cols, far, far_cols, out):
    tile = place[1]
    out[:32, :] = (
        own[:32, :]
        + dot_left(near[:32, :], near_cols[...])
        + dot_left(far[:32, :], far_cols[...])
    )
    out[32:48, :] = (
        own[32:48, :] + move_bins(near, tile, place[3]) + move_bins(far, tile, place[5])
    )


def loss_kernel(
    place,
    own,
    near,
    far,
    own_cols,
    taps,
    features_hbm,
    w_probe_hbm,
    loss_out,
    map_grad,
    parts,
    token_grad,
    nine,
    features,
    w_probe,
    sems,
):
    copies = [
        pltpu.make_async_copy(features_hbm, features, sems.at[0]),
        pltpu.make_async_copy(w_probe_hbm, w_probe, sems.at[1]),
    ]
    for copy in copies:
        copy.start()
    seq, tile = place[0], place[1]
    own_rows = row_weights(seq, seq)
    depth = jnp.zeros((32, 256), F32)
    bins = jnp.zeros((32, 256), F32)
    for block, source in ((own, seq), (near, place[2]), (far, place[4])):
        depth = depth + dot_right(row_weights(seq, source), block[:32, :])
        move = pick(
            (32, 16),
            lambda i: (i >> 4) * 1024 + seq * 8 - 3 + (i & 15),
            lambda j: (j >> 3) * 1024 + source * 8 + (j & 7),
        )
        bins = bins + dot(move, block[32:48, :].astype(BF16))
    target = (bins + 0.5) * (4.0 / NBINS) - 2.0
    error = depth - target
    loss = error * error
    for f in range(2):
        loss_out[f] = loss[f * 16 + 3 : f * 16 + 11, 3:163]
    y = lax.broadcasted_iota(jnp.int32, (32, 256), 0) & 15
    x = lax.broadcasted_iota(jnp.int32, (32, 256), 1)
    row = seq * 8 - 3 + y
    col = tile * 160 - 3 + x
    valid = (y < 14) & (x < 166) & (row >= 0) & (row < FULL_ROWS) & (col >= 0) & (col < FULL_COLS)
    grad = jnp.where(valid, 2.0 * error, 0.0)
    narrow = dot_left(dot_right(own_rows, grad, TN), own_cols[...], NT)
    for g in range(4):
        for b in range(3):
            token_grad[b * 8 : (b + 1) * 8, g * COLS : (g + 1) * COLS] = narrow[
                g * 8 : (g + 1) * 8, b * 128 : b * 128 + COLS
            ]
    grads = token_grad[...]
    map_grad[...] = lax.dot_general(
        grads, taps[...], TN, precision=PRECISE, preferred_element_type=F32
    ).astype(BF16)
    for copy in copies:
        copy.wait()
    high, low = halves(grads)
    feature_grad = jnp.dot(high, features[...], preferred_element_type=F32) + jnp.dot(
        low, features[...], preferred_element_type=F32
    )
    high, low = halves(feature_grad)
    probe = w_probe[...].astype(BF16)
    refine = dot(high, probe) + dot(low, probe)
    nine[...] = jnp.zeros_like(nine)
    for b in range(3):
        nine[b * 3 : (b + 1) * 3, :P_SIZE] = refine[b * 8 : b * 8 + 3]
        nine[b * 3 : (b + 1) * 3, P_SIZE:] = feature_grad[b * 8 : b * 8 + 3]
    every = nine[:, :P_SIZE]
    for j in range(16):
        own = nine[:, P_SIZE + j * 72 : P_SIZE + (j + 1) * 72]
        parts[j] = jnp.concatenate([every, own, jnp.zeros((16, 56), F32)], 1).astype(BF16)


def plane_sum_kernel(parts, out):
    total = jnp.sum(parts[...].astype(F32), axis=0)
    every = total[:, :P_SIZE]
    for z in range(8):
        own = total[:, P_SIZE + z * 9 : P_SIZE + (z + 1) * 9]
        out[z] = jnp.concatenate([every, own, jnp.zeros((16, 119), F32)], 1).astype(BF16)


def adam_step(grad, moment, second):
    new_moment = BETA_ONE * moment + (1.0 - BETA_ONE) * grad
    new_second = BETA_TWO * second + (1.0 - BETA_TWO) * grad * grad
    return (
        new_moment
        / (1.0 - BETA_ONE**STEP)
        / (jnp.sqrt(new_second / (1.0 - BETA_TWO**STEP)) + ADAM_EPS)
    )


def step_kernel(
    parts, w_refine, mom_probe, var_probe, mom_refine, var_refine, probe_out, refine_out, taps
):
    total = jnp.sum(parts[...].astype(F32), axis=0)
    taps[...] = jnp.zeros_like(taps)
    for a in range(3):
        for b in range(3):
            i = b * 3 + a
            taps[i : i + 1] = w_refine[a, b : b + 1]
            refine_out[a, b : b + 1] = adam_step(
                total[i : i + 1, :P_SIZE], mom_refine[a, b : b + 1], var_refine[a, b : b + 1]
            )
    probe_grad = lax.dot_general(
        total[:, P_SIZE:], taps[...], TN, precision=PRECISE, preferred_element_type=F32
    )
    probe_out[...] = adam_step(probe_grad[:9], mom_probe[...], var_probe[...])


def body(
    query_act,
    key_act,
    value_act,
    residual,
    gate_scale,
    w_out,
    w_probe,
    w_refine,
    depth_bins,
    mom_probe,
    var_probe,
    mom_refine,
    var_refine,
):
    seq = lax.axis_index(SEQ)
    tile = lax.axis_index(TILE)
    odd_seq = seq & 1
    odd_tile = tile & 1
    far_seq = seq + 2 * odd_seq - 1
    far_tile = tile + 2 * odd_tile - 1
    place = jnp.stack([seq, tile, seq ^ 1, tile ^ 1, far_seq, far_tile]).astype(jnp.int32)

    taps = jnp.pad(w_refine.transpose(1, 0, 2), ((0, 0), (0, 5), (0, 0))).reshape(24, P_SIZE)
    def split(act):
        return act.reshape(SEQ_COUNT, 1, 2, COLS * HD)

    sent = jnp.concatenate([split(query_act), split(key_act), split(value_act)], axis=1)
    here = lax.all_to_all(sent, SEQ, split_axis=0, concat_axis=0, tiled=True)
    queries = here[:, 0].reshape(ROWS, COLS * HD)
    own_kv = jnp.stack([here[:, i].reshape(ROWS, COLS * HD) for i in (1, 2)])
    swap_core = [(0, 1), (1, 0)]
    z_kv = lax.ppermute(own_kv, "z_hi", swap_core)
    core_kv = lax.ppermute(own_kv, "core", swap_core)
    query_rows, acc = attend(True, False, queries, own_kv)
    acc = attend(False, False, query_rows, core_kv, acc, unrolled=False)
    z_kv, acc = lax.optimization_barrier((z_kv, acc))
    z_core_kv = lax.ppermute(z_kv, "core", swap_core)
    acc = attend(False, False, query_rows, z_kv, acc, unrolled=False)
    attended = attend(False, True, query_rows, z_core_kv, acc)
    attended, w_probe_later = lax.optimization_barrier((attended, w_probe))
    tap_weights = call(
        weights_kernel,
        jax.ShapeDtypeStruct((48, D), BF16),
        (w_probe_later, taps),
        flops=2 * 72 * P_SIZE * D,
        bytes_accessed=4 * P_SIZE * D,
        limit=16,
    )
    merged = lax.all_to_all(
        attended.reshape(SEQ_COUNT, 2, COLS * HD), SEQ, split_axis=0, concat_axis=0, tiled=True
    ).reshape(ROWS, COLS * HD)

    features, tap_maps = call(
        features_kernel,
        [jax.ShapeDtypeStruct((160, D), BF16), jax.ShapeDtypeStruct((48, 384), F32)],
        (
            merged,
            residual.reshape(160, D),
            gate_scale.reshape(1, D),
            w_out,
            tap_weights,
            depth_bins.reshape(16, 160),
        ),
        [
            pltpu.VMEM((TOKENS, 128), F32),
            pltpu.VMEM((160, D), F32),
            pltpu.VMEM((16, 160), jnp.int32),
            pltpu.VMEM((160, D), BF16),
            pltpu.SemaphoreType.DMA((2,)),
        ],
        limit=24,
        left=(5,),
        left_out=(0,),
    )
    tile_far = [(1, 2), (2, 1)]
    seq_near = [(i, i ^ 1) for i in range(SEQ_COUNT)]
    seq_far = [(i, i + 2 * (i & 1) - 1) for i in range(1, SEQ_COUNT - 1)]
    map_far = lax.ppermute(tap_maps, TILE, tile_far)
    cols = jax.ShapeDtypeStruct((384, 256), BF16)
    wide, own_cols, near_cols, far_cols = call(
        widen_own_kernel,
        [jax.ShapeDtypeStruct((48, 256), F32), cols, cols, cols],
        (place, tap_maps),
        limit=16,
    )
    near_maps, wide = lax.optimization_barrier((tap_maps, wide))
    map_near = lax.ppermute(near_maps, "core", swap_core)
    wide = call(
        widen_kernel,
        jax.ShapeDtypeStruct((48, 256), F32),
        (place, wide, map_near, near_cols, map_far, far_cols),
        limit=16,
    )
    wide_far = lax.ppermute(wide, SEQ, seq_far)
    wide_near = lax.ppermute(wide, SEQ, seq_near)
    loss_map, map_grad, parts = call(
        loss_kernel,
        [
            jax.ShapeDtypeStruct((2, 8, 160), F32),
            jax.ShapeDtypeStruct((160, P_SIZE), BF16),
            jax.ShapeDtypeStruct((16, 16, 384), BF16),
        ],
        (place, wide, wide_near, wide_far, own_cols, taps, features, w_probe),
        [
            pltpu.VMEM((24, 160), F32),
            pltpu.VMEM((16, P_SIZE + D), F32),
            pltpu.VMEM((160, D), BF16),
            pltpu.VMEM((D, P_SIZE), F32),
            pltpu.SemaphoreType.DMA((2,)),
        ],
        limit=16,
        left=(6, 7),
    )
    parts = lax.all_to_all(parts, PLANE, split_axis=0, concat_axis=0, tiled=True)
    parts = call(plane_sum_kernel, jax.ShapeDtypeStruct((8, 16, 384), BF16), (parts,), limit=16)
    parts = lax.all_to_all(parts, COLUMN, split_axis=0, concat_axis=0, tiled=True)
    probe_step, refine_step = call(
        step_kernel,
        [
            jax.ShapeDtypeStruct((9, P_SIZE), F32),
            jax.ShapeDtypeStruct((3, 3, P_SIZE), F32),
        ],
        (parts, w_refine, mom_probe, var_probe, mom_refine, var_refine),
        [pltpu.VMEM((16, P_SIZE), F32)],
        limit=16,
    )
    return (loss_map, map_grad.reshape(2, 2, COLS, P_SIZE), probe_step, refine_step)


def solution(mesh):
    fine = Mesh(mesh.devices.reshape(4, 4, 2, 2, 2), ("y", "x", "z_lo", "z_hi", "core"))
    slab = (*SEQ, *TILE)
    in_specs = (
        P(None, None, SEQ, TILE),
        P(None, None, SEQ, TILE),
        P(None, None, SEQ, TILE),
        P(None, SEQ, TILE, None),
        P(),
        P(),
        P(),
        P(),
        P(None, SEQ, TILE),
        P(slab, None),
        P(slab, None),
        P(),
        P(),
    )
    out_specs = (
        P(None, SEQ, TILE),
        P(None, SEQ, TILE, None),
        P(slab, None),
        P(),
    )
    return jax.shard_map(body, mesh=fine, in_specs=in_specs, out_specs=out_specs, check_vma=False)
```
